512 devices in a mesh: tower: 2 (over core), blk: 128 (over x, y_hi, z), mdl: 2 (over y_lo).
Axes of the slice: x: 4, y: 4 (y_hi: 2, y_lo: 2; y = y_hi * 2 + y_lo), z: 16, core: 2. Of those that a mesh axis runs over, the one named last changes fastest.
Arguments:
- embeddings: bfloat16 [2, 1024, 4096], P('tower', 'blk', 'mdl'), may hold values from -120 to 120
- pos_index: int32 [1024, 4], P('blk'), may hold values from 0 to 1023
- pos_count: int32 [1024], P('blk'), may hold values from 1 to 4
- hidden_in: bfloat16 [2, 1024, 4096], P('tower', 'blk', 'mdl'), may hold values from -6 to 6
- w_gate: bfloat16 [2, 14336, 4096], P('tower', 'blk', 'mdl'), may hold values from -0.09375 to 0.09375
- w_up: bfloat16 [2, 14336, 4096], P('tower', 'blk', 'mdl'), may hold values from -0.09375 to 0.09375
- w_down: bfloat16 [2, 14336, 4096], P('tower', 'blk', 'mdl'), may hold values from -0.046875 to 0.046875
Outputs:
- emb_grad: float32 [2, 1024, 4096], P('tower', 'blk', 'mdl')
- grad_gate: bfloat16 [2, 14336, 4096], P('tower', 'blk', 'mdl')
- grad_up: bfloat16 [2, 14336, 4096], P('tower', 'blk', 'mdl')
- grad_down: bfloat16 [2, 14336, 4096], P('tower', 'blk', 'mdl')
The draws below stay inside these ranges and needn't reach their ends.
Inputs may be any that keep to these rules, and one draw needn't show every extreme that they name: `pos_index`: only the first pos_count slots of a goal's list are used; a list may name a premise more than once.
All inputs are finite; a program needn't handle non-finite values.
Results may differ from the reference program's by a relative error of at most 0.011.
Values may be sent and summed in bfloat16 or wider, within the bound.
A program may use at most 64 MiB of HBM per device.

```python
import math
import jax
import jax.numpy as jnp
from jax import lax

D = 4096
FF = 14336
ROWS = 8
SEQ = 128
KPOS = 4
NE = 1024
TOKENS = 1024
N_BLK = 128


def draw_embeddings(key, part):
    key = jax.random.fold_in(key, 11)
    key_base, key_scale = jax.random.split(key, 2)
    log_scale = jax.random.uniform(key_scale, (2, NE, 1), jnp.float32, math.log(0.5), math.log(2.0))
    row_scale = jnp.exp(log_scale)
    base_rows = jnp.clip(jax.random.normal(key_base, (2, NE, D), jnp.float32), -6.0, 6.0)
    scaled = base_rows * row_scale
    goal_rows = scaled[0]
    premise_rows = scaled[1]
    return jnp.clip(jnp.stack([goal_rows, premise_rows]), -120.0, 120.0).astype(jnp.bfloat16)


def place_ends(entries, key, smallest, top_value):
    place = [jax.random.randint(jax.random.fold_in(key, axis), (), 0, length) for axis, length in enumerate(entries.shape)]
    widest = entries.shape.index(max(entries.shape))
    beside = place[:widest] + [(place[widest] + 1) % entries.shape[widest]] + place[widest + 1:]
    return entries.at[tuple(place)].set(smallest).at[tuple(beside)].set(top_value)


def steps_of(own_key, extent, pieces, smallest, largest):
    def one(dim, shards_of):
        steps = jax.random.uniform(jax.random.fold_in(jax.random.fold_in(own_key, 6), dim), (shards_of,), jnp.float32, smallest / len(pieces), largest / len(pieces))
        return jnp.repeat(jnp.exp(steps), extent[dim] // shards_of).reshape((-1,) + (1,) * (len(extent) - dim - 1))

    factor_of = one(*pieces[0])
    for cut in pieces[1:]:
        factor_of = factor_of * one(*cut)
    return factor_of


def normal_values(stream_key, extent, scale, most, cuts=(), held_as=jnp.bfloat16):
    gain = steps_of(stream_key, extent, cuts, -0.22, 0.18) if cuts else 1.0
    entries = jax.random.normal(stream_key, extent, jnp.float32) * scale * gain
    return jnp.minimum(jnp.maximum(entries, -most), most).astype(held_as)


def setup_inputs(seed: int = 0) -> dict:
    key_of = jax.random.split(jax.random.key(seed), 8)
    embeddings = draw_embeddings(jax.random.fold_in(key_of[7], 71), 0)
    pos_index = place_ends(jax.random.randint(key_of[1], (NE, KPOS), 0, NE), jax.random.fold_in(key_of[1], 1), 0, NE - 1).astype(jnp.int32)
    pos_count = place_ends(jax.random.randint(key_of[2], (NE,), 1, KPOS + 1), jax.random.fold_in(key_of[2], 1), 1, KPOS).astype(jnp.int32)
    hidden_in = normal_values(key_of[3], (2, TOKENS, D), 1.0, 6.0, ((0, 2), (1, 128), (2, 2)))
    w_gate = normal_values(key_of[4], (2, FF, D), D ** -0.5, 0.09375, ((0, 2), (1, 128), (2, 2)))
    w_up = normal_values(key_of[5], (2, FF, D), D ** -0.5, 0.09375, ((0, 2), (1, 128), (2, 2)))
    w_down = normal_values(key_of[6], (2, FF, D), FF ** -0.5, 0.046875, ((0, 2), (1, 128), (2, 2)))
    return dict(embeddings=embeddings, pos_index=pos_index, pos_count=pos_count, hidden_in=hidden_in, w_gate=w_gate, w_up=w_up, w_down=w_down)


LOSS_SCALE = 256.0


def positive_table(index_rows, count_rows, column_ids):
    slot_ids = jnp.arange(KPOS, dtype=jnp.int32)
    live_slots = slot_ids[None, :, None] < count_rows[:, None, None]
    matched = (index_rows[:, :, None] == column_ids[None, None, :]) & live_slots
    hits = jnp.sum(jnp.where(matched, jnp.float32(1.0), jnp.float32(0.0)), axis=1)
    return hits / count_rows[:, None].astype(jnp.float32)


def reference(embeddings, pos_index, pos_count, hidden_in, w_gate, w_up, w_down):
    score_scale = D ** -0.5
    grad_scale = LOSS_SCALE * score_scale
    goals = embeddings[0]
    premises = embeddings[1]
    column_ids = jnp.arange(NE, dtype=jnp.int32)
    goal_blocks = goals.reshape(N_BLK, ROWS, D)
    index_blocks = pos_index.reshape(N_BLK, ROWS, KPOS)
    count_blocks = pos_count.reshape(N_BLK, ROWS)

    def block_step(running, block_in):
        goal_rows, index_rows, count_rows = block_in
        scores = jnp.dot(goal_rows, premises.T, preferred_element_type=jnp.float32) * score_scale
        row_top = jnp.max(scores, axis=1, keepdims=True)
        goal_lse = row_top[:, 0] + jnp.log(jnp.sum(jnp.exp(scores - row_top), axis=1))
        weights = positive_table(index_rows, count_rows, column_ids)
        coefficient = (jnp.exp(scores - goal_lse[:, None]) - weights).astype(jnp.bfloat16)
        goal_grad = grad_scale * jnp.dot(coefficient, premises, preferred_element_type=jnp.float32)
        running = running + jnp.dot(coefficient.T, goal_rows, preferred_element_type=jnp.float32)
        return running, goal_grad

    premise_sum, goal_grads = lax.scan(block_step, jnp.zeros((NE, D), jnp.float32), (goal_blocks, index_blocks, count_blocks))
    emb_grad = jnp.stack([goal_grads.reshape(NE, D), grad_scale * premise_sum])

    gate_list = []
    up_list = []
    down_list = []
    for tower_id in range(2):
        tokens = hidden_in[tower_id]
        gate = jnp.dot(tokens, w_gate[tower_id].T, preferred_element_type=jnp.float32)
        up_value = jnp.dot(tokens, w_up[tower_id].T, preferred_element_type=jnp.float32)
        sigmoid_gate = jax.nn.sigmoid(gate)
        activated = gate * sigmoid_gate
        hidden = (activated * up_value).astype(jnp.bfloat16)
        row_grad = (emb_grad[tower_id, :ROWS] / SEQ).astype(jnp.bfloat16)
        out_grad = jnp.repeat(row_grad, SEQ, axis=0)
        hidden_grad = jnp.dot(out_grad, w_down[tower_id].T, preferred_element_type=jnp.float32)
        slope = sigmoid_gate * (1.0 + gate * (1.0 - sigmoid_gate))
        gate_grad = (hidden_grad * up_value * slope).astype(jnp.bfloat16)
        up_grad = (hidden_grad * activated).astype(jnp.bfloat16)
        gate_list.append(jnp.dot(gate_grad.T, tokens, preferred_element_type=jnp.float32).astype(jnp.bfloat16))
        up_list.append(jnp.dot(up_grad.T, tokens, preferred_element_type=jnp.float32).astype(jnp.bfloat16))
        down_list.append(jnp.dot(hidden.T, out_grad, preferred_element_type=jnp.float32).astype(jnp.bfloat16))
    return (emb_grad, jnp.stack(gate_list), jnp.stack(up_list), jnp.stack(down_list))
```

```python
import functools

import jax
import jax.numpy as jnp
from jax import lax
from jax.experimental import pallas as pl
from jax.experimental.pallas import tpu as pltpu
from jax.sharding import PartitionSpec as P

D = 4096
SEQ = 128
KPOS = 4
LOSS_SCALE = 256.0
SCORE_SCALE = D ** (-0.5)
GRAD_SCALE = LOSS_SCALE * SCORE_SCALE

F32 = jnp.float32
BF16 = jnp.bfloat16
NT = (((1,), (1,)), ((), ()))
TN = (((0,), (0,)), ((), ()))
NN = (((1,), (0,)), ((), ()))

W = 2048
EXT = W + 128
U = 112
NX, NYH, NZ, NZL = 4, 2, 16, 4
NG, NP = 16, 8


def dot(a, b, dims):
    return lax.dot_general(a, b, dims, preferred_element_type=F32)


def slot_right(distance):
    return 0 if distance == 0 else (15 if distance == 8 else 2 * distance - 1)


def slot_left(distance):
    return 0 if distance == 0 else (15 if distance == 8 else 2 * distance)


def thirds(value):
    a = value.astype(BF16)
    rest = value - a.astype(F32)
    b = rest.astype(BF16)
    c = (rest - b.astype(F32)).astype(BF16)
    return a, b, c


def kernel(
    emb_ref, tok_ref, wg_ref, wu_ref, wd_ref,
    eg_ref, gg_ref, gu_ref, gd_ref,
    gb, pb, tok, s_own, s_in, stats, go, rs1, r2, rs2, mbp, mbr, mb, mbp1, mbr1,
    bk_own, bk_in, gown, gsend, gin, act1, act2, pool, grads,
    e1_s, e1_r, e2_s, e2_r, fw_s, fw_r, m1_s, m1_r, l1_s, l1_r, r1_s, r1_r, r2_s, r2_r,
    mq_s, mq_r, mp_s, mp_r, ma_s, ma_r, d_s, d_r, t1_s, t1_r, t2_s, t2_r,
    zr_s, zr_r, zl_s, zl_r, gu_s, gu_r,
):
    t = lax.axis_index("tower")
    b = lax.axis_index("blk")
    m = lax.axis_index("mdl")
    x = b // 32
    yh = (b // 16) % 2
    z = b % 16
    zh = z // 4
    zl = z % 4
    xy = b // 16
    gslot = x * NZL + zl
    pslot = yh * 4 + zh

    def blk_of(x_, yh_, zh_, zl_):
        return (x_ * 2 + yh_) * 16 + zh_ * 4 + zl_

    def goal_peer(k):
        q = (gslot + k) % NG
        return blk_of(q // 4, yh, zh, q % 4)

    def premise_peer(k):
        q = (pslot + k) % NP
        return blk_of(x, q // 4, q % 4, zl)

    def copy(src, dst, ss, rs, dev):
        return pltpu.make_async_remote_copy(
            src_ref=src, dst_ref=dst, send_sem=ss, recv_sem=rs,
            device_id=dev, device_id_type=pl.DeviceIdType.MESH,
        )

    def each_role(f):
        for role in (0, 1):
            @pl.when(t == role)
            def _(role=role):
                f(role)

    barrier = pltpu.get_barrier_semaphore()
    everyone = [{"blk": goal_peer(k)} for k in range(1, NG)]
    everyone += [{"blk": premise_peer(k)} for k in range(1, NP)]
    everyone += [{"blk": xy * 16 + (z + 1) % 16}, {"blk": xy * 16 + (z + 15) % 16}]
    everyone += [{"mdl": 1 - m}, {"tower": 1 - t}]
    for dev in everyone:
        pl.semaphore_signal(barrier, inc=1, device_id=dev, device_id_type=pl.DeviceIdType.MESH)
    pl.semaphore_wait(barrier, len(everyone))

    def role_of(role):
        if role == 0:
            return gb, NX, x, zl, (lambda k: blk_of((x + k) % NX, yh, zh, zl)), (
                lambda k: blk_of(x, yh, zh, (zl + k) % 4))
        return pb, NYH, yh, zh, (lambda k: blk_of(x, (yh + k) % NYH, zh, zl)), (
            lambda k: blk_of(x, yh, (zh + k) % 4, zl))

    def e1_copy(role, k):
        buf, _, mo, mi, _, inner = role_of(role)
        return copy(emb_ref, buf.at[mo * 4 + mi], e1_s.at[k - 1], e1_r.at[k - 1], {"blk": inner(k)})

    def e1_arrival(role, k):
        buf, _, mo, mi, _, inner = role_of(role)
        return copy(emb_ref, buf.at[mo * 4 + (mi - k + 4) % 4], e1_s.at[k - 1], e1_r.at[k - 1], {"blk": inner(k)})

    def e2_copy(role, k, back=0):
        buf, no, mo, _, outer, _ = role_of(role)
        part = buf.at[pl.ds(((mo - back + no) % no) * 4, 4)]
        return copy(part, part, e2_s.at[k - 1], e2_r.at[k - 1], {"blk": outer(k)})

    def fw_copy(role, k):
        buf, no, mo, _, _, _ = role_of(role)
        part = buf.at[pl.ds(((mo - k + no) % no) * 4, 4)]
        return copy(part, part, fw_s.at[k], fw_r.at[k], {"tower": 1 - t})

    def start_e1(role):
        buf, _, mo, mi, _, _ = role_of(role)
        buf[mo * 4 + mi] = emb_ref[...]
        for k in range(1, 4):
            e1_copy(role, k).start()

    each_role(start_e1)

    tok[0, xy] = tok_ref[...]

    def t1_copy(row):
        return copy(tok_ref, tok.at[0, row], t1_s.at[0], t1_r.at[0], {"blk": blk_of(x, 1 - yh, zh, zl)})

    def t2_copy(k, back=0):
        part = tok.at[0, pl.ds(((x - back + NX) % NX) * 2, 2)]
        return copy(part, part, t2_s.at[k - 1], t2_r.at[k - 1], {"blk": blk_of((x + k) % NX, yh, zh, zl)})

    def ring_copy(step, half, right):
        slot = slot_right if right else slot_left
        rows = pl.ds(4 * half, 4)
        ss, rs = (zr_s, zr_r) if right else (zl_s, zl_r)
        nxt = (z + 1) % 16 if right else (z + 15) % 16
        return copy(
            tok.at[slot(step - 1), rows], tok.at[slot(step), rows],
            ss.at[step - 1, half], rs.at[step - 1, half], {"blk": xy * 16 + nxt},
        )

    def ring_parts(step):
        for half in (0, 1):
            for right in (True, False):
                if step < 8 or (half == 0) == right:
                    yield half, right

    def ring_start(step):
        for half, right in ring_parts(step):
            ring_copy(step, half, right).start()

    def ring_step(step):
        nxt = set(ring_parts(step + 1)) if step < 8 else set()
        for half, right in ring_parts(step):
            ring_copy(step, half, right).wait_recv()
            if (half, right) in nxt:
                ring_copy(step + 1, half, right).start()

    t1_copy(xy).start()
    t1_copy(x * 2 + 1 - yh).wait_recv()
    for k in range(1, NX):
        t2_copy(k).start()

    def start_e2(role):
        for k in range(1, 4):
            e1_arrival(role, k).wait_recv()
        for k in range(1, role_of(role)[1]):
            e2_copy(role, k).start()
        fw_copy(role, 0).start()

    each_role(start_e2)

    for k in range(1, NX):
        t2_copy(k, back=k).wait_recv()
    ring_start(1)

    def forward(role):
        for k in range(1, role_of(role)[1]):
            e2_copy(role, k, back=k).wait_recv()
            fw_copy(role, k).start()
        for k in range(role_of(1 - role)[1]):
            fw_copy(1 - role, k).wait_recv()

    each_role(forward)

    goals = gb[:, :, :W].reshape(NG * 8, W)
    premises = pb[:, :, :W].reshape(NP * 8, W)
    s_own[...] = dot(premises, goals, NT)
    m1 = copy(s_own, s_in, m1_s.at[0], m1_r.at[0], {"mdl": 1 - m})
    m1.start()

    codes = jnp.transpose(gb[:, :, W:].astype(F32).reshape(NG * 8, 128))
    count = codes[8:9]
    row = lax.broadcasted_iota(jnp.int32, (NP * 8, NG * 8), 0)
    member = row // 8
    premise_id = (blk_of(x, member // 4, member % 4, zl) * 8 + row % 8).astype(F32)
    weights = jnp.zeros((NP * 8, NG * 8), F32)
    for k in range(KPOS):
        listed = codes[k:k + 1] * 32.0 + codes[4 + k:5 + k]
        hit = (listed == premise_id) & (count > float(k))
        weights = weights + jnp.where(hit, 1.0, 0.0)
    weights = weights / count

    ring_step(1)
    m1.wait_recv()
    scores = (s_own[...] + s_in[...]) * SCORE_SCALE
    top = jnp.max(scores, axis=0, keepdims=True)
    total = jnp.sum(jnp.exp(scores - top), axis=0, keepdims=True)
    stats[0] = jnp.concatenate([top, total, jnp.zeros((6, 128), F32)], axis=0)

    def l1_copy(k):
        return copy(stats.at[0], stats.at[k], l1_s.at[k - 1], l1_r.at[k - 1], {"blk": goal_peer(k)})

    for k in range(1, NG):
        l1_copy(k).start()

    def gate_copy(c):
        return copy(gsend.at[c], gin.at[c], gu_s.at[c], gu_r.at[c], {"mdl": 1 - m})

    def gate_chunk(c):
        rows = tok[4 * c:4 * c + 4].reshape(256, W)
        g = dot(wg_ref[...], rows, NT)
        u = dot(wu_ref[...], rows, NT)
        gown[c, :U] = g
        gown[c, U:] = u
        gsend[c, :U] = g.astype(BF16)
        gsend[c, U:] = u.astype(BF16)
        gate_copy(c).start()

    def spread(dtype):
        lane = lax.broadcasted_iota(jnp.int32, (8, 256), 1)
        sub = lax.broadcasted_iota(jnp.int32, (8, 256), 0)
        return jnp.where((lane // 8) % 8 == sub, 1.0, 0.0).astype(dtype)

    def act_chunk(c):
        gate_copy(c).wait_recv()
        g = gown[c, :U] + gin[c, :U].astype(F32)
        u = gown[c, U:] + gin[c, U:].astype(F32)
        s = 1.0 / (1.0 + jnp.exp(-g))
        a = g * s
        hidden = (a * u).astype(BF16)
        act1[c] = u * (s * (1.0 + g * (1.0 - s)))
        act2[c] = a
        part = dot(spread(BF16), hidden, NT)
        if c == 0:
            pool[:, :U] = part
        else:
            pool[:, :U] += part

    ring_step(2)
    gate_chunk(0)

    for k in range(1, NG):
        l1_copy(k).wait_recv()
    tops = [stats[k, 0:1] for k in range(NG)]
    peak = functools.reduce(jnp.maximum, tops)
    mass = functools.reduce(lambda p, q: p + q, [stats[k, 1:2] * jnp.exp(tops[k] - peak) for k in range(NG)])
    lse = peak + jnp.log(mass)
    coefficient = jnp.exp(scores - lse) - weights

    def mq_copy(role, k):
        if role == 0:
            return copy(mbp.at[(gslot + k) % NG], mbr.at[k - 1], mq_s.at[k - 1], mq_r.at[k - 1], {"blk": goal_peer(k)})
        return copy(mbp1.at[(pslot + k) % NP], mbr1.at[k - 1], mq_s.at[k - 1], mq_r.at[k - 1], {"blk": premise_peer(k)})

    def r1_copy(role, k):
        _, no, mo, _, outer, _ = role_of(role)
        return copy(go.at[pl.ds(((mo + k) % no) * 4, 4)], rs1.at[k - 1], r1_s.at[k - 1], r1_r.at[k - 1], {"blk": outer(k)})

    def r2_copy(role, k):
        _, _, _, mi, _, inner = role_of(role)
        return copy(r2.at[(mi + k) % 4], rs2.at[k - 1], r2_s.at[k - 1], r2_r.at[k - 1], {"blk": inner(k)})

    def in_first(role):
        return (pslot if role == 0 else gslot) == 0

    def members(role):
        return NG if role == 0 else NP

    def start_sums(role):
        if role == 0:
            lhs = jnp.transpose(coefficient).astype(BF16)
            other = premises
        else:
            lhs = coefficient.astype(BF16)
            other = goals
        part = dot(lhs, other, NN)
        n = members(role)
        wide = W // n
        go[:n] = part.astype(BF16).reshape(n, 8, W)

        @pl.when(in_first(role))
        def _():
            target = mbp if role == 0 else mbp1
            for q in range(n):
                target[q] = part[:8, q * wide:(q + 1) * wide]
            for k in range(1, n):
                mq_copy(role, k).start()

        for k in range(1, role_of(role)[1]):
            r1_copy(role, k).start()

    each_role(start_sums)
    ring_step(3)

    def slice_of(role, q):
        wide = W // members(role)
        return mb.at[:, pl.ds(pl.multiple_of(q * wide, wide), wide)]

    def mp_copy(role, k):
        part = slice_of(role, gslot if role == 0 else pslot)
        return copy(part, part, mp_s.at[k - 1], mp_r.at[0],
                    {"blk": premise_peer(k) if role == 0 else goal_peer(k)})

    def ma_copy(role, k, back=0):
        n = members(role)
        me = gslot if role == 0 else pslot
        part = slice_of(role, (me - back + n) % n)
        return copy(part, part, ma_s.at[k - 1], ma_r.at[k - 1],
                    {"blk": goal_peer(k) if role == 0 else premise_peer(k)})

    def spread_micro(role):
        n = members(role)
        wide = W // n
        me = gslot if role == 0 else pslot
        own, got = (mbp, mbr) if role == 0 else (mbp1, mbr1)

        @pl.when(in_first(role))
        def _():
            acc = own[me]
            for k in range(1, n):
                mq_copy(role, k).wait_recv()
                acc = acc + got[k - 1]
            lo = pl.multiple_of(me * wide, wide)
            mb[:, pl.ds(lo, wide)] = ((GRAD_SCALE * acc) / SEQ).astype(BF16)
            for k in range(1, members(1 - role)):
                mp_copy(role, k).start()

        @pl.when(jnp.logical_not(in_first(role)))
        def _():
            mp_copy(role, 1).wait_recv()

        for k in range(1, n):
            ma_copy(role, k).start()

    each_role(spread_micro)

    def second_sums(role):
        _, no, mo, _, _, _ = role_of(role)
        acc = go[pl.ds(mo * 4, 4)].astype(F32)
        for k in range(1, no):
            r1_copy(role, k).wait_recv()
            acc = acc + rs1[k - 1].astype(F32)
        r2[...] = acc.astype(BF16)
        for k in range(1, 4):
            r2_copy(role, k).start()

    each_role(second_sums)
    ring_step(4)
    gate_chunk(1)

    def all_micro(role):
        for k in range(1, members(role)):
            ma_copy(role, k, back=k).wait_recv()

    each_role(all_micro)
    bk_own[:, :U] = dot(mb[...], wd_ref[...], NT)
    bk_own[:, U:] = jnp.zeros((8, 128 - U), F32)
    back = copy(bk_own, bk_in, d_s.at[0], d_r.at[0], {"mdl": 1 - m})
    back.start()
    ring_step(5)

    def last_sums(role):
        mi = role_of(role)[3]
        acc = r2[mi].astype(F32)
        for k in range(1, 4):
            r2_copy(role, k).wait_recv()
            acc = acc + rs2[k - 1].astype(F32)
        eg_ref[...] = GRAD_SCALE * acc

    each_role(last_sums)
    act_chunk(0)
    ring_step(6)
    gate_chunk(2)
    act_chunk(1)
    back.wait_recv()
    back_rows = jnp.transpose(bk_own[...] + bk_in[...])[:U]

    def back_chunk(c):
        wide = sum(dot(p, spread(BF16), NN) for p in thirds(back_rows))
        grads[:U, 256 * c:256 * c + 256] = (wide * act1[c]).astype(BF16)
        grads[U:, 256 * c:256 * c + 256] = (wide * act2[c]).astype(BF16)

    ring_step(7)
    act_chunk(2)
    for c in range(3):
        back_chunk(c)
    ring_step(8)
    gate_chunk(3)
    act_chunk(3)
    back_chunk(3)

    pool[:, U:] = jnp.zeros((8, 128 - U), F32)
    pooled = thirds(jnp.transpose(pool[...])[:U])
    gd_ref[...] = sum(dot(p, mb[...], NN) for p in pooled).astype(BF16)

    @pl.loop(0, W // 512)
    def _(j):
        cols = pl.ds(pl.multiple_of(j * 512, 512), 512)
        both = dot(grads[...], tok[:, :, :, cols].reshape(1024, 512), NN)
        gg_ref[:, cols] = both[:U].astype(BF16)
        gu_ref[:, cols] = both[U:].astype(BF16)

    def drain(role):
        n = members(role)
        for k in range(1, 4):
            e1_copy(role, k).wait_send()
            r2_copy(role, k).wait_send()
        for k in range(1, role_of(role)[1]):
            e2_copy(role, k).wait_send()
            r1_copy(role, k).wait_send()
        for k in range(role_of(role)[1]):
            fw_copy(role, k).wait_send()
        for k in range(1, n):
            ma_copy(role, k).wait_send()

        @pl.when(in_first(role))
        def _():
            for k in range(1, n):
                mq_copy(role, k).wait_send()
            for k in range(1, members(1 - role)):
                mp_copy(role, k).wait_send()

    each_role(drain)
    t1_copy(xy).wait_send()
    for k in range(1, NX):
        t2_copy(k).wait_send()
    for step in range(1, 9):
        for half, right in ring_parts(step):
            ring_copy(step, half, right).wait_send()
    m1.wait_send()
    back.wait_send()
    for k in range(1, NG):
        l1_copy(k).wait_send()
    for c in range(4):
        gate_copy(c).wait_send()


def on_device(embeddings, pos_index, pos_count, hidden_in, w_gate, w_up, w_down):
    coded = jnp.concatenate([pos_index // 32, pos_index % 32, pos_count[:, None]], axis=1)
    coded = jnp.pad(coded.astype(BF16), ((0, 0), (0, 128 - coded.shape[1])))
    own = jnp.concatenate([embeddings[0], coded], axis=1)
    vmem = pl.BlockSpec(memory_space=pltpu.VMEM)
    dma = pltpu.SemaphoreType.DMA
    counts = [3, 3, 3, 3, 4, 4, 1, 1, 15, 15, 3, 3, 3, 3, 15, 15, 15, 1, 15, 15, 1, 1, 1, 1, 3, 3]
    out = pl.pallas_call(
        kernel,
        out_shape=(
            jax.ShapeDtypeStruct((8, W), F32),
            jax.ShapeDtypeStruct((U, W), BF16),
            jax.ShapeDtypeStruct((U, W), BF16),
            jax.ShapeDtypeStruct((U, W), BF16),
        ),
        in_specs=[vmem] * 5,
        out_specs=(vmem,) * 4,
        scratch_shapes=[
            pltpu.VMEM((NG, 8, EXT), BF16),
            pltpu.VMEM((NP, 8, EXT), BF16),
            pltpu.VMEM((NZ, 8, 8, W), BF16),
            pltpu.VMEM((NP * 8, NG * 8), F32),
            pltpu.VMEM((NP * 8, NG * 8), F32),
            pltpu.VMEM((NG, 8, 128), F32),
            pltpu.VMEM((NG, 8, W), BF16),
            pltpu.VMEM((3, 4, 8, W), BF16),
            pltpu.VMEM((4, 8, W), BF16),
            pltpu.VMEM((3, 8, W), BF16),
            pltpu.VMEM((NG, 8, 128), F32),
            pltpu.VMEM((NG - 1, 8, 128), F32),
            pltpu.VMEM((8, W), BF16),
            pltpu.VMEM((NP, 8, 256), F32),
            pltpu.VMEM((NP - 1, 8, 256), F32),
            pltpu.VMEM((8, 128), F32),
            pltpu.VMEM((8, 128), F32),
            pltpu.VMEM((4, 2 * U, 256), F32),
            pltpu.VMEM((4, 2 * U, 256), BF16),
            pltpu.VMEM((4, 2 * U, 256), BF16),
            pltpu.VMEM((4, U, 256), F32),
            pltpu.VMEM((4, U, 256), F32),
            pltpu.VMEM((8, 128), F32),
            pltpu.VMEM((2 * U, 1024), BF16),
        ]
        + [dma((n,)) for n in counts]
        + [dma((8, 2))] * 4
        + [dma((4,))] * 2,
        compiler_params=pltpu.CompilerParams(
            collective_id=0, has_side_effects=True, vmem_limit_bytes=48 * 1024 * 1024
        ),
    )(own, hidden_in[0], w_gate[0], w_up[0], w_down[0])
    return tuple(v[None] for v in out)


def solution(mesh):
    wide = P("tower", "blk", "mdl")
    return jax.shard_map(
        on_device,
        mesh=mesh,
        in_specs=(wide, P("blk", None), P("blk"), wide, wide, wide, wide),
        out_specs=(wide,) * 4,
        check_vma=False,
    )
```

```python
import functools

import jax
import jax.numpy as jnp
from jax import lax
from jax.experimental import pallas as pl
from jax.experimental.pallas import tpu as pltpu
from jax.sharding import PartitionSpec as P

D = 4096
SEQ = 128
KPOS = 4
LOSS_SCALE = 256.0
SCORE_SCALE = D ** (-0.5)
GRAD_SCALE = LOSS_SCALE * SCORE_SCALE

F32 = jnp.float32
BF16 = jnp.bfloat16
NT = (((1,), (1,)), ((), ()))
NN = (((1,), (0,)), ((), ()))

W = 2048
FIRST, SECOND, THIRD = pl.ds(0, 1024), pl.ds(1024, 512), pl.ds(1536, 512)
FIRST_SECOND = pl.ds(0, 1536)
TILE = 512
U = 112
NX, NYH, NZ = 4, 2, 16
NG, NP = 16, 8


def dot(a, b, dims):
    return lax.dot_general(a, b, dims, preferred_element_type=F32)


def thirds(value):
    a = value.astype(BF16)
    rest = value - a.astype(F32)
    b = rest.astype(BF16)
    c = (rest - b.astype(F32)).astype(BF16)
    return a, b, c


def kernel(
    pos_ref, cnt_ref, emb_ref, hid_ref, wg_hbm, wu_hbm, wd_hbm,
    eg_ref, gg_ref, gu_ref, gd_ref,
    mb, pool, grads, tok, early,
    gb, pb, wg_ref, wu_ref, wd_ref, s_own, s_in, stats, go, rs1, r2, rs2, mbp, mbr, mbp1, mbr1,
    bk_own, bk_in, gown, gsend, gin, act1, act2,
    loc, e1_s, e1_r, e2_s, e2_r, fw_s, fw_r, m1_s, m1_r, l1_s, l1_r, r1_s, r1_r, r2_s, r2_r,
    mq_s, mq_r, mp_s, mp_r, ma_s, ma_r, d_s, d_r,
    za_s, za_r, zb_s, zb_r, yb_s, yb_r, xb_s, xb_r, yc_s, yc_r, xc_s, xc_r, yd_s, yd_r, xd_s, xd_r, zd_s, zd_r, gu_s, gu_r,
):
    t = lax.axis_index("tower")
    b = lax.axis_index("blk")
    m = lax.axis_index("mdl")
    xy = lax.div(b, 16)
    z = lax.rem(b, 16)
    x = lax.div(xy, 2)
    yh = lax.rem(xy, 2)
    zh = lax.div(z, 4)
    zl = lax.rem(z, 4)
    gslot = x * 4 + zl
    pslot = yh * 4 + zh

    def blk_of(x_, yh_, zh_, zl_):
        return (x_ * 2 + yh_) * 16 + zh_ * 4 + zl_

    x_at = [x] + [lax.rem(x + k, 4) for k in (1, 2, 3)]
    zl_at = [zl] + [lax.rem(zl + k, 4) for k in (1, 2, 3)]
    zh_at = [zh] + [lax.rem(zh + k, 4) for k in (1, 2, 3)]
    yh_at = [yh, 1 - yh]

    goal_ids = [blk_of(x_at[k // 4], yh, zh, zl_at[k % 4]) for k in range(NG)]
    premise_ids = [blk_of(x, yh_at[k // 4], zh_at[k % 4], zl) for k in range(NP)]
    z_ids = {d: xy * 16 + lax.rem(z + d + 16, 16) for d in (1, -1, 2, -2)}
    y_id = premise_ids[4]
    x_ids = [goal_ids[4 * k] for k in range(NX)]

    def goal_slot(k, back=False):
        o, i = k // 4, k % 4
        return x_at[(4 - o) % 4 if back else o] * 4 + zl_at[(4 - i) % 4 if back else i]

    def premise_slot(k, back=False):
        o, i = k // 4, k % 4
        return yh_at[o] * 4 + zh_at[(4 - i) % 4 if back else i]

    def copy(src, dst, ss, rs, dev):
        return pltpu.make_async_remote_copy(
            src_ref=src, dst_ref=dst, send_sem=ss, recv_sem=rs,
            device_id=dev, device_id_type=pl.DeviceIdType.MESH,
        )

    def each_role(f):
        for role in (0, 1):
            @pl.when(t == role)
            def _(role=role):
                f(role)

    def count_of(role):
        return (NG, NP)[role]

    def ids_of(role):
        return (goal_ids, premise_ids)[role]

    def slot_of(role, k, back=False):
        return (goal_slot, premise_slot)[role](k, back)

    barrier = pltpu.get_barrier_semaphore()
    everyone = [{"blk": v} for v in goal_ids[1:] + premise_ids[1:] + list(z_ids.values())]
    everyone += [{"mdl": 1 - m}, {"tower": 1 - t}]
    for dev in everyone:
        pl.semaphore_signal(barrier, inc=1, device_id=dev, device_id_type=pl.DeviceIdType.MESH)

    def own_emb(role):
        return pltpu.make_async_copy(emb_ref.at[0], (gb, pb)[role].at[slot_of(role, 0)], loc.at[0])

    own_tok = pltpu.make_async_copy(hid_ref.at[0], tok.at[0, x, yh], loc.at[1])
    own_wg = pltpu.make_async_copy(wg_hbm.at[0], wg_ref, loc.at[2])
    own_wu = pltpu.make_async_copy(wu_hbm.at[0], wu_ref, loc.at[3])
    own_wd = pltpu.make_async_copy(wd_hbm.at[0], wd_ref, loc.at[4])
    each_role(lambda role: own_emb(role).start())
    for fetch in (own_tok, own_wg, own_wu, own_wd):
        fetch.start()

    stats[0] = jnp.zeros((8, 128), F32)
    stats[0, 2:6, :8] = pos_ref[...].astype(F32)
    stats[0, 6:7, :8] = cnt_ref[...].astype(F32)
    lists = pltpu.roll(stats[0], gslot * 8, 1)
    each_role(lambda role: own_emb(role).wait())
    own_tok.wait()
    pl.semaphore_wait(barrier, len(everyone))

    def e1_copy(role, k, back=False):
        part = (gb, pb)[role].at[slot_of(role, k if back else 0, back)]
        return copy(part, part, e1_s.at[k - 1], e1_r.at[k - 1], {"blk": ids_of(role)[k]})

    def e2_copy(role, o, i, back=False):
        part = (gb, pb)[role].at[slot_of(role, 4 * o + i if back else i, True)]
        return copy(part, part, e2_s.at[o - 1, i], e2_r.at[o - 1, i], {"blk": ids_of(role)[4 * o]})

    def fw_copy(role, k):
        part = (gb, pb)[role].at[slot_of(role, k, True)]
        return copy(part, part, fw_s.at[k], fw_r.at[k], {"tower": 1 - t})

    def emb_own(role):
        for k in (2, 1, 3):
            e1_copy(role, k).start()
        for o in range(1, count_of(role) // 4):
            e2_copy(role, o, 0).start()
        fw_copy(role, 0).start()

    def emb_inner(role):
        for i in (1, 3, 2):
            e1_copy(role, i, back=True).wait_recv()
            for o in range(1, count_of(role) // 4):
                e2_copy(role, o, i).start()
            fw_copy(role, i).start()

    def emb_outer(role):
        for i in (0, 1, 3, 2):
            for o in range(1, count_of(role) // 4):
                e2_copy(role, o, i, back=True).wait_recv()
                fw_copy(role, 4 * o + i).start()
        for k in range(count_of(1 - role)):
            fw_copy(1 - role, k).wait_recv()

    def za_copy(k):
        return copy(tok.at[0, x, yh], tok.at[k, x, yh], za_s.at[k - 1], za_r.at[k - 1], {"blk": premise_ids[k]})

    zb_parts = ((0, 4, 4, 1), (0, 4, 8, -1), (0, 2, 12, 2), (0, 1, 15, -2), (3, 1, 14, -2))

    def zb_copy(i):
        first, n, there, d = zb_parts[i]
        return copy(tok.at[pl.ds(first, n), x, yh, :, FIRST_SECOND], tok.at[pl.ds(there, n), x, yh, :, FIRST_SECOND],
                    zb_s.at[i], zb_r.at[i], {"blk": z_ids[d]})

    def yd_copy(row):
        part = tok.at[pl.ds(0, 4), x, row, :, THIRD]
        return copy(part, part, yd_s.at[0], yd_r.at[0], {"blk": y_id})

    def xd_copy(k, back=False):
        part = tok.at[pl.ds(0, 4), x_at[4 - k] if back else x, :, :, THIRD]
        return copy(part, part, xd_s.at[k - 1], xd_r.at[k - 1], {"blk": x_ids[k]})

    def zd_copy(i):
        first, n, there, d = zb_parts[i]
        return copy(tok.at[pl.ds(first, n), :, :, :, THIRD], tok.at[pl.ds(there, n), :, :, :, THIRD],
                    zd_s.at[i], zd_r.at[i], {"blk": z_ids[d]})

    def yb_copy(g, row):
        part = tok.at[pl.ds(4 * g, 4), x, row, :, FIRST]
        return copy(part, part, yb_s.at[g], yb_r.at[g], {"blk": y_id})

    def xc_copy(g, k, back=False):
        part = tok.at[pl.ds(4 * g, 4), x_at[4 - k] if back else x, yh, :, SECOND]
        return copy(part, part, xc_s.at[g, k - 1], xc_r.at[g, k - 1], {"blk": x_ids[k]})

    def xb_copy(g, k, back=False):
        part = tok.at[pl.ds(4 * g, 4), x_at[4 - k] if back else x, :, :, FIRST]
        return copy(part, part, xb_s.at[g, k - 1], xb_r.at[g, k - 1], {"blk": x_ids[k]})

    def yc_copy(g, row):
        part = tok.at[pl.ds(4 * g, 4), :, row, :, SECOND]
        return copy(part, part, yc_s.at[g], yc_r.at[g], {"blk": y_id})

    def tok_first():
        for k in (2, 1, 3):
            za_copy(k).start()
        zb_copy(3).start()

    def tok_near():
        for k in (1, 3, 2):
            za_copy(k).wait_recv()
        for i in (0, 1, 2, 4):
            zb_copy(i).start()
        yd_copy(yh).start()

    def tok_wide():
        yd_copy(1 - yh).wait_recv()
        for k in (1, 3, 2):
            xd_copy(k).start()

    def tok_far():
        for k in (1, 3, 2):
            xd_copy(k, back=True).wait_recv()
        for i in range(len(zb_parts)):
            zd_copy(i).start()

    def tok_second(g):
        for i, part in enumerate(zb_parts):
            if part[2] // 4 == g:
                zb_copy(i).wait_recv()
        for k in (1, 3, 2):
            xc_copy(g, k).start()
        yb_copy(g, yh).start()

    def tok_third(g):
        yb_copy(g, 1 - yh).wait_recv()
        for k in (1, 3, 2):
            xb_copy(g, k).start()
        for k in (1, 3, 2):
            xc_copy(g, k, back=True).wait_recv()
        yc_copy(g, yh).start()

    def tok_last(g):
        for k in (1, 3, 2):
            xb_copy(g, k, back=True).wait_recv()
        yc_copy(g, 1 - yh).wait_recv()
        for i, part in enumerate(zb_parts):
            if part[2] // 4 == g:
                zd_copy(i).wait_recv()

    each_role(emb_own)
    tok_first()
    each_role(emb_inner)
    tok_near()
    tok_second(0)
    each_role(emb_outer)
    tok_wide()

    goals = gb[...].reshape(NG * 8, W)
    premises = pb[...].reshape(NP * 8, W)
    s_own[...] = dot(premises, goals, NT)
    m1 = copy(s_own, s_in, m1_s.at[0], m1_r.at[0], {"mdl": 1 - m})
    m1.start()
    tok_second(1)

    m1.wait_recv()
    scores = (s_own[...] + s_in[...]) * SCORE_SCALE
    top = jnp.max(scores, axis=0, keepdims=True)
    total = jnp.sum(jnp.exp(scores - top), axis=0, keepdims=True)
    line = lax.broadcasted_iota(jnp.int32, (8, 128), 0)
    stats[0] = jnp.where(line == 0, top, jnp.where(line == 1, total, lists))

    def l1_copy(k):
        return copy(stats.at[0], stats.at[k], l1_s.at[k - 1], l1_r.at[k - 1], {"blk": goal_ids[k]})

    for k in range(1, NG):
        l1_copy(k).start()
    tok_second(2)
    tok_far()
    tok_third(0)

    def gate_copy(c):
        return copy(gsend.at[c], gin.at[c], gu_s.at[c], gu_r.at[c], {"mdl": 1 - m})

    def gate_chunk(c):
        rows = tok[4 * c:4 * c + 4].reshape(256, W)
        for lo, w in ((0, wg_ref), (U, wu_ref)):
            v = dot(w[...], rows, NT)
            gown[c, lo:lo + U] = v
            gsend[c, lo:lo + U] = v.astype(BF16)
        gate_copy(c).start()

    def spread(dtype):
        lane = lax.broadcasted_iota(jnp.int32, (8, 256), 1)
        sub = lax.broadcasted_iota(jnp.int32, (8, 256), 0)
        return jnp.where(lax.rem(lax.div(lane, 8), 8) == sub, 1.0, 0.0).astype(dtype)

    def act_chunk(c):
        gate_copy(c).wait_recv()
        g = gown[c, :U] + gin[c, :U].astype(F32)
        u = gown[c, U:] + gin[c, U:].astype(F32)
        s = 1.0 / (1.0 + jnp.exp(-g))
        a = g * s
        hidden = (a * u).astype(BF16)
        act1[c] = u * (s * (1.0 + g * (1.0 - s)))
        act2[c] = a
        part = dot(spread(BF16), hidden, NT)
        if c == 0:
            pool[:, U:] = jnp.zeros((8, 128 - U), F32)
            pool[:, :U] = part
        else:
            pool[:, :U] += part

    for k in range(1, NG):
        l1_copy(k).wait_recv()
    tops = [stats[k, 0:1] for k in range(NG)]
    peak = functools.reduce(jnp.maximum, tops)
    mass = functools.reduce(lambda p, q: p + q, [stats[k, 1:2] * jnp.exp(tops[k] - peak) for k in range(NG)])
    lse = peak + jnp.log(mass)
    codes = functools.reduce(lambda p, q: p + q, [stats[k] for k in range(NG)])
    count = codes[6:7]
    row = lax.broadcasted_iota(jnp.int32, (NP * 8, NG * 8), 0)
    member = lax.div(row, 8)
    premise_id = (blk_of(x, lax.div(member, 4), lax.rem(member, 4), zl) * 8 + lax.rem(row, 8)).astype(F32)
    weights = jnp.zeros((NP * 8, NG * 8), F32)
    for k in range(KPOS):
        hit = (codes[2 + k:3 + k] == premise_id) & (count > float(k))
        weights = weights + jnp.where(hit, 1.0, 0.0)
    coefficient = jnp.exp(scores - lse) - weights / count

    def mq_copy(role, k):
        src, dst = ((mbp, mbr), (mbp1, mbr1))[role]
        return copy(src.at[slot_of(role, k)], dst.at[k - 1], mq_s.at[k - 1], mq_r.at[k - 1], {"blk": ids_of(role)[k]})

    def r1_copy(role, k):
        first = (x_at, yh_at)[role][k] * 4
        return copy(go.at[pl.ds(first, 4)], rs1.at[k - 1], r1_s.at[k - 1], r1_r.at[k - 1], {"blk": ids_of(role)[4 * k]})

    def r2_copy(role, k):
        return copy(r2.at[(zl_at, zh_at)[role][k]], rs2.at[k - 1], r2_s.at[k - 1], r2_r.at[k - 1], {"blk": ids_of(role)[k]})

    def in_first(role):
        return (pslot, gslot)[role] == 0

    def start_sums(role):
        if role == 0:
            lhs = jnp.transpose(coefficient).astype(BF16)
            other = premises
        else:
            lhs = coefficient.astype(BF16)
            other = goals
        n = count_of(role)
        wide = W // n

        @pl.when(in_first(role))
        def _():
            target = (mbp, mbp1)[role]
            head = dot(lhs[:8], other, NN)
            for q in range(n):
                target[q] = head[:, q * wide:(q + 1) * wide]
            for k in range(1, n):
                mq_copy(role, k).start()

        go[:n] = dot(lhs, other, NN).astype(BF16).reshape(n, 8, W)
        for k in range(1, n // 4):
            r1_copy(role, k).start()

    each_role(start_sums)
    tok_second(3)
    tok_third(1)

    def slice_of(role, q):
        wide = W // count_of(role)
        return mb.at[:, pl.ds(pl.multiple_of(q * wide, wide), wide)]

    def mp_copy(role, k):
        part = slice_of(role, slot_of(role, 0))
        return copy(part, part, mp_s.at[k - 1], mp_r.at[0], {"blk": ids_of(1 - role)[k]})

    def ma_copy(role, k, back=False):
        part = slice_of(role, slot_of(role, k if back else 0, back))
        return copy(part, part, ma_s.at[k - 1], ma_r.at[k - 1], {"blk": ids_of(role)[k]})

    def spread_micro(role):
        n = count_of(role)
        wide = W // n
        me = slot_of(role, 0)
        own, got = ((mbp, mbr), (mbp1, mbr1))[role]

        @pl.when(in_first(role))
        def _():
            acc = own[me]
            for k in range(1, n):
                mq_copy(role, k).wait_recv()
                acc = acc + got[k - 1]
            mb[:, pl.ds(pl.multiple_of(me * wide, wide), wide)] = ((GRAD_SCALE * acc) / SEQ).astype(BF16)
            for k in range(1, count_of(1 - role)):
                mp_copy(role, k).start()

        @pl.when(jnp.logical_not(in_first(role)))
        def _():
            mp_copy(role, 1).wait_recv()

        for k in range(1, n):
            ma_copy(role, k).start()

    each_role(spread_micro)
    tok_third(2)

    def second_sums(role):
        acc = go[pl.ds((x, yh)[role] * 4, 4)].astype(F32)
        for k in range(1, count_of(role) // 4):
            r1_copy(role, k).wait_recv()
            acc = acc + rs1[k - 1].astype(F32)
        r2[...] = acc.astype(BF16)
        for k in range(1, 4):
            r2_copy(role, k).start()

    each_role(second_sums)
    own_wg.wait()
    own_wu.wait()
    own_wd.wait()
    tok_last(0)
    gate_chunk(0)

    def all_micro(role):
        for k in range(1, count_of(role)):
            ma_copy(role, k, back=True).wait_recv()

    each_role(all_micro)
    bk_own[:, :U] = dot(mb[...], wd_ref[...], NT)
    bk_own[:, U:] = jnp.zeros((8, 128 - U), F32)
    back = copy(bk_own, bk_in, d_s.at[0], d_r.at[0], {"mdl": 1 - m})
    back.start()
    tok_third(3)
    tok_last(1)
    gate_chunk(1)

    def last_sums(role):
        acc = r2[(zl, zh)[role]].astype(F32)
        for k in range(1, 4):
            r2_copy(role, k).wait_recv()
            acc = acc + rs2[k - 1].astype(F32)
        eg_ref[...] = GRAD_SCALE * acc

    each_role(last_sums)
    act_chunk(0)
    back.wait_recv()
    back_rows = thirds(jnp.transpose(bk_own[...] + bk_in[...])[:U])

    def back_chunk(c):
        wide = sum(dot(p, spread(BF16), NN) for p in back_rows)
        grads[:U, 256 * c:256 * c + 256] = (wide * act1[c]).astype(BF16)
        grads[U:, 256 * c:256 * c + 256] = (wide * act2[c]).astype(BF16)

    tok_last(2)
    gate_chunk(2)
    act_chunk(1)
    back_chunk(0)
    back_chunk(1)
    tok_last(3)
    gate_chunk(3)
    act_chunk(2)
    back_chunk(2)
    for j in range(W // TILE):
        cols = pl.ds(j * TILE, TILE)
        early[j] = dot(grads[:, :768], tok[:12, :, :, :, cols].reshape(768, TILE), NN)
    act_chunk(3)
    back_chunk(3)
    pooled = thirds(jnp.transpose(pool[...])[:U])
    gd_ref[...] = sum(dot(p, mb[...], NN) for p in pooled).astype(BF16)
    for j in range(W // TILE):
        cols = pl.ds(j * TILE, TILE)
        both = early[j] + dot(grads[:, 768:], tok[12:, :, :, :, cols].reshape(256, TILE), NN)
        gg_ref[:, cols] = both[:U].astype(BF16)
        gu_ref[:, cols] = both[U:].astype(BF16)

    def drain(role):
        n = count_of(role)
        for k in range(1, 4):
            e1_copy(role, k).wait_send()
            r2_copy(role, k).wait_send()
        for o in range(1, n // 4):
            for i in range(4):
                e2_copy(role, o, i).wait_send()
            r1_copy(role, o).wait_send()
        for k in range(n):
            fw_copy(role, k).wait_send()
        for k in range(1, n):
            ma_copy(role, k).wait_send()

        @pl.when(in_first(role))
        def _():
            for k in range(1, n):
                mq_copy(role, k).wait_send()
            for k in range(1, count_of(1 - role)):
                mp_copy(role, k).wait_send()

    each_role(drain)
    for k in (1, 2, 3):
        za_copy(k).wait_send()
        xd_copy(k).wait_send()
    for i in range(len(zb_parts)):
        zb_copy(i).wait_send()
        zd_copy(i).wait_send()
    yd_copy(yh).wait_send()
    for g in range(4):
        yb_copy(g, yh).wait_send()
        yc_copy(g, yh).wait_send()
        for k in (1, 2, 3):
            xb_copy(g, k).wait_send()
            xc_copy(g, k).wait_send()
    m1.wait_send()
    back.wait_send()
    for k in range(1, NG):
        l1_copy(k).wait_send()
    for c in range(4):
        gate_copy(c).wait_send()


def hand_over(eg, gg, gu, gd, eg_out, gg_out, gu_out, gd_out, sem):
    copies = [pltpu.make_async_copy(eg, eg_out.at[0], sem.at[0])]
    for j in range(W // TILE):
        cols = pl.ds(j * TILE, TILE)
        for v, out in ((gg, gg_out), (gu, gu_out), (gd, gd_out)):
            copies.append(pltpu.make_async_copy(v.at[:, cols], out.at[0, :, cols], sem.at[len(copies)]))
    for c in copies:
        c.start()
    for c in copies:
        c.wait()


def on_device(embeddings, pos_index, pos_count, hidden_in, w_gate, w_up, w_down):
    vmem = pl.BlockSpec(memory_space=pltpu.VMEM)
    hbm = pl.BlockSpec(memory_space=pltpu.HBM)
    dma = pltpu.SemaphoreType.DMA
    shapes = [(5,), (3,), (3,), (3, 4), (3, 4), (16,), (16,), (1,), (1,), (15,), (15,), (3,), (3,), (3,), (3,)]
    shapes += [(15,), (15,), (15,), (1,), (15,), (15,), (1,), (1,)]
    shapes += [(3,), (3,), (5,), (5,), (4,), (4,), (4, 3), (4, 3), (4,), (4,), (4, 3), (4, 3), (1,), (1,), (3,), (3,), (5,), (5,), (4,), (4,)]
    results = (jax.ShapeDtypeStruct((1, 8, W), F32),) + (jax.ShapeDtypeStruct((1, U, W), BF16),) * 3
    parts = pl.pallas_call(
        kernel,
        out_shape=tuple(pltpu.VMEM(v.shape[1:], v.dtype) for v in results),
        in_specs=[vmem] * 2 + [hbm] * 5,
        out_specs=(vmem,) * 4,
        scratch_shapes=[
            pltpu.VMEM((8, W), BF16),
            pltpu.VMEM((8, 128), F32),
            pltpu.VMEM((2 * U, 1024), BF16),
            pltpu.VMEM((NZ, NX, NYH, 8, W), BF16),
            pltpu.VMEM((W // TILE, 2 * U, TILE), F32),
            pltpu.VMEM((NG, 8, W), BF16),
            pltpu.VMEM((NP, 8, W), BF16),
            pltpu.VMEM((U, W), BF16),
            pltpu.VMEM((U, W), BF16),
            pltpu.VMEM((U, W), BF16),
            pltpu.VMEM((NP * 8, NG * 8), F32),
            pltpu.VMEM((NP * 8, NG * 8), F32),
            pltpu.VMEM((NG, 8, 128), F32),
            pltpu.VMEM((NG, 8, W), BF16),
            pltpu.VMEM((3, 4, 8, W), BF16),
            pltpu.VMEM((4, 8, W), BF16),
            pltpu.VMEM((3, 8, W), BF16),
            pltpu.VMEM((NG, 8, 128), F32),
            pltpu.VMEM((NG - 1, 8, 128), F32),
            pltpu.VMEM((NP, 8, 256), F32),
            pltpu.VMEM((NP - 1, 8, 256), F32),
            pltpu.VMEM((8, 128), F32),
            pltpu.VMEM((8, 128), F32),
            pltpu.VMEM((4, 2 * U, 256), F32),
            pltpu.VMEM((4, 2 * U, 256), BF16),
            pltpu.VMEM((4, 2 * U, 256), BF16),
            pltpu.VMEM((4, U, 256), F32),
            pltpu.VMEM((4, U, 256), F32),
        ]
        + [dma(s) for s in shapes],
        compiler_params=pltpu.CompilerParams(
            collective_id=0, has_side_effects=True, vmem_limit_bytes=60 * 1024 * 1024
        ),
    )(pos_index.T, pos_count[None], embeddings, hidden_in, w_gate, w_up, w_down)
    return pl.pallas_call(
        hand_over,
        out_shape=results,
        in_specs=[vmem] * 4,
        out_specs=(hbm,) * 4,
        scratch_shapes=[dma((13,))],
    )(*parts)


def solution(mesh):
    wide = P("tower", "blk", "mdl")
    return jax.shard_map(
        on_device,
        mesh=mesh,
        in_specs=(wide, P("blk", None), P("blk"), wide, wide, wide, wide),
        out_specs=(wide,) * 4,
        check_vma=False,
    )
```

```python
import functools

import jax
import jax.numpy as jnp
from jax import lax
from jax.experimental import pallas as pl
from jax.experimental.pallas import tpu as pltpu
from jax.sharding import PartitionSpec as P

D = 4096
SEQ = 128
KPOS = 4
LOSS_SCALE = 256.0
SCORE_SCALE = D ** (-0.5)
GRAD_SCALE = LOSS_SCALE * SCORE_SCALE

F32 = jnp.float32
BF16 = jnp.bfloat16
NT = (((1,), (1,)), ((), ()))
NN = (((1,), (0,)), ((), ()))

W = 2048
FIRST, SECOND, THIRD = pl.ds(0, 1024), pl.ds(1024, 512), pl.ds(1536, 512)
FIRST_SECOND = pl.ds(0, 1536)
TILE = 512
U = 112
NX, NYH, NZ = 4, 2, 16
NG, NP = 16, 8


def dot(a, b, dims):
    return lax.dot_general(a, b, dims, preferred_element_type=F32)


def thirds(value):
    a = value.astype(BF16)
    rest = value - a.astype(F32)
    b = rest.astype(BF16)
    c = (rest - b.astype(F32)).astype(BF16)
    return a, b, c


def kernel(
    pos_ref, cnt_ref, emb_ref, hid_ref, wg_hbm, wu_hbm, wd_hbm,
    eg_ref, gg_ref, gu_ref, gd_ref,
    mb, pool, grads, tok, early,
    gb, pb, wgu_ref, wd_ref, s_own, s_in, stats, go, rs1, r2, rs2, mbp, mbr, mbp1, mbr1,
    bk_own, bk_in, gown, gsend, gin, act1, act2,
    loc, e1_s, e1_r, e2_s, e2_r, fw_s, fw_r, m1_s, m1_r, l1_s, l1_r, r1_s, r1_r, r2_s, r2_r,
    mq_s, mq_r, mp_s, mp_r, ma_s, ma_r, d_s, d_r,
    za_s, za_r, zb_s, zb_r, yb_s, yb_r, xb_s, xb_r, yc_s, yc_r, xc_s, xc_r, yd_s, yd_r, xd_s, xd_r, zd_s, zd_r, gu_s, gu_r,
):
    t = lax.axis_index("tower")
    b = lax.axis_index("blk")
    m = lax.axis_index("mdl")
    xy = lax.div(b, 16)
    z = lax.rem(b, 16)
    x = lax.div(xy, 2)
    yh = lax.rem(xy, 2)
    zh = lax.div(z, 4)
    zl = lax.rem(z, 4)
    gslot = x * 4 + zl
    pslot = yh * 4 + zh

    def blk_of(x_, yh_, zh_, zl_):
        return (x_ * 2 + yh_) * 16 + zh_ * 4 + zl_

    x_at = [x] + [lax.rem(x + k, 4) for k in (1, 2, 3)]
    zl_at = [zl] + [lax.rem(zl + k, 4) for k in (1, 2, 3)]
    zh_at = [zh] + [lax.rem(zh + k, 4) for k in (1, 2, 3)]
    yh_at = [yh, 1 - yh]

    goal_ids = [blk_of(x_at[k // 4], yh, zh, zl_at[k % 4]) for k in range(NG)]
    premise_ids = [blk_of(x, yh_at[k // 4], zh_at[k % 4], zl) for k in range(NP)]
    z_ids = {d: xy * 16 + lax.rem(z + d + 16, 16) for d in (1, -1, 2, -2)}
    y_id = premise_ids[4]
    x_ids = [goal_ids[4 * k] for k in range(NX)]

    def goal_slot(k, back=False):
        o, i = k // 4, k % 4
        return x_at[(4 - o) % 4 if back else o] * 4 + zl_at[(4 - i) % 4 if back else i]

    def premise_slot(k, back=False):
        o, i = k // 4, k % 4
        return yh_at[o] * 4 + zh_at[(4 - i) % 4 if back else i]

    def copy(src, dst, ss, rs, dev):
        return pltpu.make_async_remote_copy(
            src_ref=src, dst_ref=dst, send_sem=ss, recv_sem=rs,
            device_id=dev, device_id_type=pl.DeviceIdType.MESH,
        )

    def each_role(f):
        for role in (0, 1):
            @pl.when(t == role)
            def _(role=role):
                f(role)

    def count_of(role):
        return (NG, NP)[role]

    def ids_of(role):
        return (goal_ids, premise_ids)[role]

    def slot_of(role, k, back=False):
        return (goal_slot, premise_slot)[role](k, back)

    barrier = pltpu.get_barrier_semaphore()
    everyone = [{"blk": v} for v in goal_ids[1:] + premise_ids[1:] + list(z_ids.values())]
    everyone += [{"mdl": 1 - m}, {"tower": 1 - t}]
    for dev in everyone:
        pl.semaphore_signal(barrier, inc=1, device_id=dev, device_id_type=pl.DeviceIdType.MESH)

    def own_emb(role):
        return pltpu.make_async_copy(emb_ref.at[0], (gb, pb)[role].at[slot_of(role, 0)], loc.at[0])

    own_tok = pltpu.make_async_copy(hid_ref.at[0], tok.at[0, x, yh], loc.at[1])
    own_wg = pltpu.make_async_copy(wg_hbm.at[0], wgu_ref.at[pl.ds(0, U)], loc.at[2])
    own_wu = pltpu.make_async_copy(wu_hbm.at[0], wgu_ref.at[pl.ds(U, U)], loc.at[3])
    own_wd = pltpu.make_async_copy(wd_hbm.at[0], wd_ref, loc.at[4])
    each_role(lambda role: own_emb(role).start())
    for fetch in (own_tok, own_wg, own_wu, own_wd):
        fetch.start()

    stats[0] = jnp.zeros((8, 128), F32)
    stats[0, 2:6, :8] = pos_ref[...].astype(F32)
    stats[0, 6:7, :8] = cnt_ref[...].astype(F32)
    lists = pltpu.roll(stats[0], gslot * 8, 1)
    each_role(lambda role: own_emb(role).wait())
    own_tok.wait()
    pl.semaphore_wait(barrier, len(everyone))

    def e1_copy(role, k, back=False):
        part = (gb, pb)[role].at[slot_of(role, k if back else 0, back)]
        return copy(part, part, e1_s.at[k - 1], e1_r.at[k - 1], {"blk": ids_of(role)[k]})

    def e2_copy(role, o, i, back=False):
        part = (gb, pb)[role].at[slot_of(role, 4 * o + i if back else i, True)]
        return copy(part, part, e2_s.at[o - 1, i], e2_r.at[o - 1, i], {"blk": ids_of(role)[4 * o]})

    def fw_copy(role, k):
        part = (gb, pb)[role].at[slot_of(role, k, True)]
        return copy(part, part, fw_s.at[k], fw_r.at[k], {"tower": 1 - t})

    def emb_own(role):
        for k in (2, 1, 3):
            e1_copy(role, k).start()
        for o in range(1, count_of(role) // 4):
            e2_copy(role, o, 0).start()
        fw_copy(role, 0).start()

    def emb_inner(role):
        for i in (1, 3, 2):
            e1_copy(role, i, back=True).wait_recv()
            for o in range(1, count_of(role) // 4):
                e2_copy(role, o, i).start()
            fw_copy(role, i).start()

    def emb_outer(role):
        for i in (0, 1, 3, 2):
            for o in range(1, count_of(role) // 4):
                e2_copy(role, o, i, back=True).wait_recv()
                fw_copy(role, 4 * o + i).start()
        for k in range(count_of(1 - role)):
            fw_copy(1 - role, k).wait_recv()

    def za_copy(k):
        return copy(tok.at[0, x, yh], tok.at[k, x, yh], za_s.at[k - 1], za_r.at[k - 1], {"blk": premise_ids[k]})

    zb_parts = ((0, 4, 4, 1), (0, 4, 8, -1), (0, 2, 12, 2), (0, 1, 15, -2), (3, 1, 14, -2))

    def zb_copy(i):
        first, n, there, d = zb_parts[i]
        return copy(tok.at[pl.ds(first, n), x, yh, :, FIRST_SECOND], tok.at[pl.ds(there, n), x, yh, :, FIRST_SECOND],
                    zb_s.at[i], zb_r.at[i], {"blk": z_ids[d]})

    def yd_copy(row):
        part = tok.at[pl.ds(0, 4), x, row, :, THIRD]
        return copy(part, part, yd_s.at[0], yd_r.at[0], {"blk": y_id})

    def xd_copy(k, back=False):
        part = tok.at[pl.ds(0, 4), x_at[4 - k] if back else x, :, :, THIRD]
        return copy(part, part, xd_s.at[k - 1], xd_r.at[k - 1], {"blk": x_ids[k]})

    def zd_copy(i):
        first, n, there, d = zb_parts[i]
        return copy(tok.at[pl.ds(first, n), :, :, :, THIRD], tok.at[pl.ds(there, n), :, :, :, THIRD],
                    zd_s.at[i], zd_r.at[i], {"blk": z_ids[d]})

    def yb_copy(g, row):
        part = tok.at[pl.ds(4 * g, 4), x, row, :, FIRST]
        return copy(part, part, yb_s.at[g], yb_r.at[g], {"blk": y_id})

    def xc_copy(g, k, back=False):
        part = tok.at[pl.ds(4 * g, 4), x_at[4 - k] if back else x, yh, :, SECOND]
        return copy(part, part, xc_s.at[g, k - 1], xc_r.at[g, k - 1], {"blk": x_ids[k]})

    def xb_copy(g, k, back=False):
        part = tok.at[pl.ds(4 * g, 4), x_at[4 - k] if back else x, :, :, FIRST]
        return copy(part, part, xb_s.at[g, k - 1], xb_r.at[g, k - 1], {"blk": x_ids[k]})

    def yc_copy(g, row):
        part = tok.at[pl.ds(4 * g, 4), :, row, :, SECOND]
        return copy(part, part, yc_s.at[g], yc_r.at[g], {"blk": y_id})

    def tok_first():
        for k in (2, 1, 3):
            za_copy(k).start()
        zb_copy(3).start()

    def tok_near():
        for k in (1, 3, 2):
            za_copy(k).wait_recv()
        for i in (0, 1, 2, 4):
            zb_copy(i).start()
        yd_copy(yh).start()

    def tok_wide():
        yd_copy(1 - yh).wait_recv()
        for k in (1, 3, 2):
            xd_copy(k).start()

    def tok_far():
        for k in (1, 3, 2):
            xd_copy(k, back=True).wait_recv()
        for i in range(len(zb_parts)):
            zd_copy(i).start()

    def tok_second(g):
        for i, part in enumerate(zb_parts):
            if part[2] // 4 == g:
                zb_copy(i).wait_recv()
        for k in (1, 3, 2):
            xc_copy(g, k).start()
        yb_copy(g, yh).start()

    def tok_third(g):
        yb_copy(g, 1 - yh).wait_recv()
        for k in (1, 3, 2):
            xb_copy(g, k).start()
        for k in (1, 3, 2):
            xc_copy(g, k, back=True).wait_recv()
        yc_copy(g, yh).start()

    def tok_last(g):
        for k in (1, 3, 2):
            xb_copy(g, k, back=True).wait_recv()
        yc_copy(g, 1 - yh).wait_recv()
        for i, part in enumerate(zb_parts):
            if part[2] // 4 == g:
                zd_copy(i).wait_recv()

    each_role(emb_own)
    tok_first()
    each_role(emb_inner)
    tok_near()
    tok_second(0)
    each_role(emb_outer)
    tok_wide()

    goals = gb[...].reshape(NG * 8, W)
    premises = pb[...].reshape(NP * 8, W)
    s_own[...] = dot(premises, goals, NT)
    m1 = copy(s_own, s_in, m1_s.at[0], m1_r.at[0], {"mdl": 1 - m})
    m1.start()

    m1.wait_recv()
    scores = (s_own[...] + s_in[...]) * SCORE_SCALE
    top = jnp.max(scores, axis=0, keepdims=True)
    total = jnp.sum(jnp.exp(scores - top), axis=0, keepdims=True)
    line = lax.broadcasted_iota(jnp.int32, (8, 128), 0)
    stats[0] = jnp.where(line == 0, top, jnp.where(line == 1, total, lists))

    def l1_copy(k):
        return copy(stats.at[0], stats.at[k], l1_s.at[k - 1], l1_r.at[k - 1], {"blk": goal_ids[k]})

    for k in range(1, NG):
        l1_copy(k).start()
    tok_second(1)
    tok_second(2)
    tok_third(0)

    def gate_copy(c):
        return copy(gsend.at[c], gin.at[c], gu_s.at[c], gu_r.at[c], {"mdl": 1 - m})

    def gate_chunk(c):
        rows = tok[4 * c:4 * c + 4].reshape(256, W)
        both = dot(wgu_ref[...], rows, NT)
        gown[c] = both
        gsend[c] = both.astype(BF16)
        gate_copy(c).start()

    def spread(rows):
        lane = lax.broadcasted_iota(jnp.int32, (rows, 256), 1)
        sub = lax.broadcasted_iota(jnp.int32, (rows, 256), 0)
        return jnp.where(lax.rem(lax.div(lane, 8), 8) == lax.rem(sub, 8), 1.0, 0.0).astype(BF16)

    def act_chunk(c):
        gate_copy(c).wait_recv()
        g = gown[c, :U] + gin[c, :U].astype(F32)
        u = gown[c, U:] + gin[c, U:].astype(F32)
        s = 1.0 / (1.0 + jnp.exp(-g))
        a = g * s
        hidden = (a * u).astype(BF16)
        act1[c] = u * (s * (1.0 + g * (1.0 - s)))
        act2[c] = a
        part = dot(spread(8), hidden, NT)
        if c == 0:
            pool[:, U:] = jnp.zeros((8, 128 - U), F32)
            pool[:, :U] = part
        else:
            pool[:, :U] += part

    for k in range(1, NG):
        l1_copy(k).wait_recv()
    tops = [stats[k, 0:1] for k in range(NG)]
    peak = functools.reduce(jnp.maximum, tops)
    mass = functools.reduce(lambda p, q: p + q, [stats[k, 1:2] * jnp.exp(tops[k] - peak) for k in range(NG)])
    lse = peak + jnp.log(mass)
    codes = functools.reduce(lambda p, q: p + q, [stats[k] for k in range(NG)])
    count = codes[6:7]
    row = lax.broadcasted_iota(jnp.int32, (NP * 8, NG * 8), 0)
    member = lax.div(row, 8)
    premise_id = (blk_of(x, lax.div(member, 4), lax.rem(member, 4), zl) * 8 + lax.rem(row, 8)).astype(F32)
    weights = jnp.zeros((NP * 8, NG * 8), F32)
    for k in range(KPOS):
        hit = (codes[2 + k:3 + k] == premise_id) & (count > float(k))
        weights = weights + jnp.where(hit, 1.0, 0.0)
    coefficient = jnp.exp(scores - lse) - weights / count

    def mq_copy(role, k):
        src, dst = ((mbp, mbr), (mbp1, mbr1))[role]
        return copy(src.at[slot_of(role, k)], dst.at[k - 1], mq_s.at[k - 1], mq_r.at[k - 1], {"blk": ids_of(role)[k]})

    def r1_copy(role, k):
        first = (x_at, yh_at)[role][k] * 4
        return copy(go.at[pl.ds(first, 4)], rs1.at[k - 1], r1_s.at[k - 1], r1_r.at[k - 1], {"blk": ids_of(role)[4 * k]})

    def r2_copy(role, k):
        return copy(r2.at[(zl_at, zh_at)[role][k]], rs2.at[k - 1], r2_s.at[k - 1], r2_r.at[k - 1], {"blk": ids_of(role)[k]})

    def in_first(role):
        return (pslot, gslot)[role] == 0

    def start_sums(role):
        if role == 0:
            lhs = jnp.transpose(coefficient).astype(BF16)
            other = premises
        else:
            lhs = coefficient.astype(BF16)
            other = goals
        n = count_of(role)
        wide = W // n

        @pl.when(in_first(role))
        def _():
            target = (mbp, mbp1)[role]
            head = dot(lhs[:8], other, NN)
            for q in range(n):
                target[q] = head[:, q * wide:(q + 1) * wide]
            for k in range(1, n):
                mq_copy(role, k).start()

        go[:n] = dot(lhs, other, NN).astype(BF16).reshape(n, 8, W)
        for k in range(1, n // 4):
            r1_copy(role, k).start()

    each_role(start_sums)
    tok_second(3)
    tok_far()
    tok_third(1)

    def slice_of(role, q):
        wide = W // count_of(role)
        return mb.at[:, pl.ds(pl.multiple_of(q * wide, wide), wide)]

    def mp_copy(role, k):
        part = slice_of(role, slot_of(role, 0))
        return copy(part, part, mp_s.at[k - 1], mp_r.at[0], {"blk": ids_of(1 - role)[k]})

    def ma_copy(role, k, back=False):
        part = slice_of(role, slot_of(role, k if back else 0, back))
        return copy(part, part, ma_s.at[k - 1], ma_r.at[k - 1], {"blk": ids_of(role)[k]})

    def spread_micro(role):
        n = count_of(role)
        wide = W // n
        me = slot_of(role, 0)
        own, got = ((mbp, mbr), (mbp1, mbr1))[role]

        @pl.when(in_first(role))
        def _():
            acc = own[me]
            for k in range(1, n):
                mq_copy(role, k).wait_recv()
                acc = acc + got[k - 1]
            mb[:, pl.ds(pl.multiple_of(me * wide, wide), wide)] = ((GRAD_SCALE * acc) / SEQ).astype(BF16)
            for k in range(1, count_of(1 - role)):
                mp_copy(role, k).start()

        @pl.when(jnp.logical_not(in_first(role)))
        def _():
            mp_copy(role, 1).wait_recv()

        for k in range(1, n):
            ma_copy(role, k).start()

    each_role(spread_micro)
    tok_third(2)

    def second_sums(role):
        acc = go[pl.ds((x, yh)[role] * 4, 4)].astype(F32)
        for k in range(1, count_of(role) // 4):
            r1_copy(role, k).wait_recv()
            acc = acc + rs1[k - 1].astype(F32)
        r2[...] = acc.astype(BF16)
        for k in range(1, 4):
            r2_copy(role, k).start()

    each_role(second_sums)
    own_wg.wait()
    own_wu.wait()
    own_wd.wait()
    tok_last(0)
    gate_chunk(0)

    def all_micro(role):
        for k in range(1, count_of(role)):
            ma_copy(role, k, back=True).wait_recv()

    each_role(all_micro)
    bk_own[:, :U] = dot(mb[...], wd_ref[...], NT)
    bk_own[:, U:] = jnp.zeros((8, 128 - U), F32)
    back = copy(bk_own, bk_in, d_s.at[0], d_r.at[0], {"mdl": 1 - m})
    back.start()
    tok_third(3)
    tok_last(1)
    gate_chunk(1)

    def last_sums(role):
        acc = r2[(zl, zh)[role]].astype(F32)
        for k in range(1, 4):
            r2_copy(role, k).wait_recv()
            acc = acc + rs2[k - 1].astype(F32)
        eg_ref[...] = GRAD_SCALE * acc

    each_role(last_sums)
    act_chunk(0)
    back.wait_recv()
    back_rows = jnp.concatenate(thirds(jnp.transpose(bk_own[...] + bk_in[...])[:U]), axis=1)

    def back_chunk(c):
        wide = dot(back_rows, spread(24), NN)
        grads[:U, 256 * c:256 * c + 256] = (wide * act1[c]).astype(BF16)
        grads[U:, 256 * c:256 * c + 256] = (wide * act2[c]).astype(BF16)

    tok_last(2)
    gate_chunk(2)
    act_chunk(1)
    back_chunk(0)
    back_chunk(1)
    tok_last(3)
    gate_chunk(3)
    act_chunk(2)
    back_chunk(2)
    for j in range(W // TILE):
        cols = pl.ds(j * TILE, TILE)
        early[j] = dot(grads[:, :768], tok[:12, :, :, :, cols].reshape(768, TILE), NN)
    def drain(role):
        n = count_of(role)
        for k in range(1, 4):
            e1_copy(role, k).wait_send()
            r2_copy(role, k).wait_send()
        for o in range(1, n // 4):
            for i in range(4):
                e2_copy(role, o, i).wait_send()
            r1_copy(role, o).wait_send()
        for k in range(n):
            fw_copy(role, k).wait_send()
        for k in range(1, n):
            ma_copy(role, k).wait_send()

        @pl.when(in_first(role))
        def _():
            for k in range(1, n):
                mq_copy(role, k).wait_send()
            for k in range(1, count_of(1 - role)):
                mp_copy(role, k).wait_send()

    each_role(drain)
    for k in (1, 2, 3):
        za_copy(k).wait_send()
        xd_copy(k).wait_send()
    for i in range(len(zb_parts)):
        zb_copy(i).wait_send()
        zd_copy(i).wait_send()
    yd_copy(yh).wait_send()
    for g in range(4):
        yb_copy(g, yh).wait_send()
        yc_copy(g, yh).wait_send()
        for k in (1, 2, 3):
            xb_copy(g, k).wait_send()
            xc_copy(g, k).wait_send()
    m1.wait_send()
    back.wait_send()
    for k in range(1, NG):
        l1_copy(k).wait_send()
    for c in range(3):
        gate_copy(c).wait_send()

    act_chunk(3)
    back_chunk(3)
    pooled = jnp.concatenate(thirds(jnp.transpose(pool[...])[:U]), axis=1)
    gd_ref[...] = dot(pooled, jnp.concatenate([mb[...]] * 3, axis=0), NN).astype(BF16)
    for j in range(W // TILE):
        cols = pl.ds(j * TILE, TILE)
        both = early[j] + dot(grads[:, 768:], tok[12:, :, :, :, cols].reshape(256, TILE), NN)
        gg_ref[:, cols] = both[:U].astype(BF16)
        gu_ref[:, cols] = both[U:].astype(BF16)

    gate_copy(3).wait_send()


def hand_over(eg, gg, gu, gd, eg_out, gg_out, gu_out, gd_out, sem):
    copies = [pltpu.make_async_copy(eg, eg_out.at[0], sem.at[0])]
    for j in range(W // TILE):
        cols = pl.ds(j * TILE, TILE)
        for v, out in ((gg, gg_out), (gu, gu_out), (gd, gd_out)):
            copies.append(pltpu.make_async_copy(v.at[:, cols], out.at[0, :, cols], sem.at[len(copies)]))
    for c in copies:
        c.start()
    for c in copies:
        c.wait()


def on_device(embeddings, pos_index, pos_count, hidden_in, w_gate, w_up, w_down):
    vmem = pl.BlockSpec(memory_space=pltpu.VMEM)
    hbm = pl.BlockSpec(memory_space=pltpu.HBM)
    dma = pltpu.SemaphoreType.DMA
    shapes = [(5,), (3,), (3,), (3, 4), (3, 4), (16,), (16,), (1,), (1,), (15,), (15,), (3,), (3,), (3,), (3,)]
    shapes += [(15,), (15,), (15,), (1,), (15,), (15,), (1,), (1,)]
    shapes += [(3,), (3,), (5,), (5,), (4,), (4,), (4, 3), (4, 3), (4,), (4,), (4, 3), (4, 3), (1,), (1,), (3,), (3,), (5,), (5,), (4,), (4,)]
    results = (jax.ShapeDtypeStruct((1, 8, W), F32),) + (jax.ShapeDtypeStruct((1, U, W), BF16),) * 3
    parts = pl.pallas_call(
        kernel,
        out_shape=tuple(pltpu.VMEM(v.shape[1:], v.dtype) for v in results),
        in_specs=[vmem] * 2 + [hbm] * 5,
        out_specs=(vmem,) * 4,
        scratch_shapes=[
            pltpu.VMEM((8, W), BF16),
            pltpu.VMEM((8, 128), F32),
            pltpu.VMEM((2 * U, 1024), BF16),
            pltpu.VMEM((NZ, NX, NYH, 8, W), BF16),
            pltpu.VMEM((W // TILE, 2 * U, TILE), F32),
            pltpu.VMEM((NG, 8, W), BF16),
            pltpu.VMEM((NP, 8, W), BF16),
            pltpu.VMEM((2 * U, W), BF16),
            pltpu.VMEM((U, W), BF16),
            pltpu.VMEM((NP * 8, NG * 8), F32),
            pltpu.VMEM((NP * 8, NG * 8), F32),
            pltpu.VMEM((NG, 8, 128), F32),
            pltpu.VMEM((NG, 8, W), BF16),
            pltpu.VMEM((3, 4, 8, W), BF16),
            pltpu.VMEM((4, 8, W), BF16),
            pltpu.VMEM((3, 8, W), BF16),
            pltpu.VMEM((NG, 8, 128), F32),
            pltpu.VMEM((NG - 1, 8, 128), F32),
            pltpu.VMEM((NP, 8, 256), F32),
            pltpu.VMEM((NP - 1, 8, 256), F32),
            pltpu.VMEM((8, 128), F32),
            pltpu.VMEM((8, 128), F32),
            pltpu.VMEM((4, 2 * U, 256), F32),
            pltpu.VMEM((4, 2 * U, 256), BF16),
            pltpu.VMEM((4, 2 * U, 256), BF16),
            pltpu.VMEM((4, U, 256), F32),
            pltpu.VMEM((4, U, 256), F32),
        ]
        + [dma(s) for s in shapes],
        compiler_params=pltpu.CompilerParams(
            collective_id=0, has_side_effects=True, vmem_limit_bytes=60 * 1024 * 1024
        ),
    )(pos_index.T, pos_count[None], embeddings, hidden_in, w_gate, w_up, w_down)
    return pl.pallas_call(
        hand_over,
        out_shape=results,
        in_specs=[vmem] * 4,
        out_specs=(hbm,) * 4,
        scratch_shapes=[dma((13,))],
    )(*parts)


def solution(mesh):
    wide = P("tower", "blk", "mdl")
    return jax.shard_map(
        on_device,
        mesh=mesh,
        in_specs=(wide, P("blk", None), P("blk"), wide, wide, wide, wide),
        out_specs=(wide,) * 4,
        check_vma=False,
    )
```

```python
import functools

import jax
import jax.numpy as jnp
from jax import lax
from jax.experimental import pallas as pl
from jax.experimental.pallas import tpu as pltpu
from jax.sharding import PartitionSpec as P

D = 4096
SEQ = 128
KPOS = 4
LOSS_SCALE = 256.0
SCORE_SCALE = D ** (-0.5)
GRAD_SCALE = LOSS_SCALE * SCORE_SCALE

F32 = jnp.float32
BF16 = jnp.bfloat16
NT = (((1,), (1,)), ((), ()))
NN = (((1,), (0,)), ((), ()))

W = 2048
FIRST, SECOND, THIRD = pl.ds(0, 1024), pl.ds(1024, 640), pl.ds(1664, 384)
FIRST_SECOND = pl.ds(0, 1664)
TILE = 512
U = 112
NX, NYH, NZ = 4, 2, 16
NG, NP = 16, 8


def dot(a, b, dims):
    return lax.dot_general(a, b, dims, preferred_element_type=F32)


def thirds(value):
    a = value.astype(BF16)
    rest = value - a.astype(F32)
    b = rest.astype(BF16)
    c = (rest - b.astype(F32)).astype(BF16)
    return a, b, c


def kernel(
    pos_ref, cnt_ref, emb_ref, hid_ref, wg_hbm, wu_hbm, wd_hbm,
    eg_ref, gg_ref, gu_ref, gd_ref,
    mb, pool, grads, tok, early,
    gb, pb, wgu_ref, wd_ref, s_own, s_in, stats, go, rs1, r2, rs2, mbp, mbr, mbp1, mbr1,
    bk_own, bk_in, gown, gsend, gin, act1, act2,
    loc, e1_s, e1_r, e2_s, e2_r, fw_s, fw_r, m1_s, m1_r, l1_s, l1_r, r1_s, r1_r, r2_s, r2_r,
    mq_s, mq_r, mp_s, mp_r, ma_s, ma_r, d_s, d_r,
    za_s, za_r, zb_s, zb_r, yb_s, yb_r, xb_s, xb_r, yc_s, yc_r, xc_s, xc_r, yd_s, yd_r, xd_s, xd_r, zd_s, zd_r, gu_s, gu_r,
):
    t = lax.axis_index("tower")
    b = lax.axis_index("blk")
    m = lax.axis_index("mdl")
    xy = lax.div(b, 16)
    z = lax.rem(b, 16)
    x = lax.div(xy, 2)
    yh = lax.rem(xy, 2)
    zh = lax.div(z, 4)
    zl = lax.rem(z, 4)
    gslot = x * 4 + zl
    pslot = yh * 4 + zh

    def blk_of(x_, yh_, zh_, zl_):
        return (x_ * 2 + yh_) * 16 + zh_ * 4 + zl_

    x_at = [x] + [lax.rem(x + k, 4) for k in (1, 2, 3)]
    zl_at = [zl] + [lax.rem(zl + k, 4) for k in (1, 2, 3)]
    zh_at = [zh] + [lax.rem(zh + k, 4) for k in (1, 2, 3)]
    yh_at = [yh, 1 - yh]

    goal_ids = [blk_of(x_at[k // 4], yh, zh, zl_at[k % 4]) for k in range(NG)]
    premise_ids = [blk_of(x, yh_at[k // 4], zh_at[k % 4], zl) for k in range(NP)]
    z_ids = {d: xy * 16 + lax.rem(z + d + 16, 16) for d in (1, -1, 2, -2)}
    y_id = premise_ids[4]
    x_ids = [goal_ids[4 * k] for k in range(NX)]

    def goal_slot(k, back=False):
        o, i = k // 4, k % 4
        return x_at[(4 - o) % 4 if back else o] * 4 + zl_at[(4 - i) % 4 if back else i]

    def premise_slot(k, back=False):
        o, i = k // 4, k % 4
        return yh_at[o] * 4 + zh_at[(4 - i) % 4 if back else i]

    def copy(src, dst, ss, rs, dev):
        return pltpu.make_async_remote_copy(
            src_ref=src, dst_ref=dst, send_sem=ss, recv_sem=rs,
            device_id=dev, device_id_type=pl.DeviceIdType.MESH,
        )

    def each_role(f):
        for role in (0, 1):
            @pl.when(t == role)
            def _(role=role):
                f(role)

    def count_of(role):
        return (NG, NP)[role]

    def ids_of(role):
        return (goal_ids, premise_ids)[role]

    def slot_of(role, k, back=False):
        return (goal_slot, premise_slot)[role](k, back)

    barrier = pltpu.get_barrier_semaphore()
    everyone = [{"blk": v} for v in goal_ids[1:] + premise_ids[1:] + list(z_ids.values())]
    everyone += [{"mdl": 1 - m}, {"tower": 1 - t}]
    for dev in everyone:
        pl.semaphore_signal(barrier, inc=1, device_id=dev, device_id_type=pl.DeviceIdType.MESH)

    def own_emb(role):
        return pltpu.make_async_copy(emb_ref.at[0], (gb, pb)[role].at[slot_of(role, 0)], loc.at[0])

    own_tok = pltpu.make_async_copy(hid_ref.at[0], tok.at[0, x, yh], loc.at[1])
    own_wg = pltpu.make_async_copy(wg_hbm.at[0], wgu_ref.at[pl.ds(0, U)], loc.at[2])
    own_wu = pltpu.make_async_copy(wu_hbm.at[0], wgu_ref.at[pl.ds(U, U)], loc.at[3])
    own_wd = pltpu.make_async_copy(wd_hbm.at[0], wd_ref, loc.at[4])
    each_role(lambda role: own_emb(role).start())
    for fetch in (own_tok, own_wg, own_wu, own_wd):
        fetch.start()

    stats[0] = jnp.zeros((8, 128), F32)
    stats[0, 2:6, :8] = pos_ref[...].astype(F32)
    stats[0, 6:7, :8] = cnt_ref[...].astype(F32)
    lists = pltpu.roll(stats[0], gslot * 8, 1)
    each_role(lambda role: own_emb(role).wait())
    own_tok.wait()
    pl.semaphore_wait(barrier, len(everyone))

    def e1_copy(role, k, back=False):
        part = (gb, pb)[role].at[slot_of(role, k if back else 0, back)]
        return copy(part, part, e1_s.at[k - 1], e1_r.at[k - 1], {"blk": ids_of(role)[k]})

    def e2_copy(role, o, i, back=False):
        part = (gb, pb)[role].at[slot_of(role, 4 * o + i if back else i, True)]
        return copy(part, part, e2_s.at[o - 1, i], e2_r.at[o - 1, i], {"blk": ids_of(role)[4 * o]})

    def fw_copy(role, k):
        part = (gb, pb)[role].at[slot_of(role, k, True)]
        return copy(part, part, fw_s.at[k], fw_r.at[k], {"tower": 1 - t})

    def emb_own(role):
        for k in (2, 1, 3):
            e1_copy(role, k).start()
        for o in range(1, count_of(role) // 4):
            e2_copy(role, o, 0).start()
        fw_copy(role, 0).start()

    def emb_inner(role):
        for i in (1, 3, 2):
            e1_copy(role, i, back=True).wait_recv()
            for o in range(1, count_of(role) // 4):
                e2_copy(role, o, i).start()
            fw_copy(role, i).start()

    def emb_outer(role):
        for i in (0, 1, 3, 2):
            for o in range(1, count_of(role) // 4):
                e2_copy(role, o, i, back=True).wait_recv()
                fw_copy(role, 4 * o + i).start()
        for k in range(count_of(1 - role)):
            fw_copy(1 - role, k).wait_recv()

    def za_copy(k):
        return copy(tok.at[0, x, yh], tok.at[k, x, yh], za_s.at[k - 1], za_r.at[k - 1], {"blk": premise_ids[k]})

    zb_parts = ((0, 4, 4, 1), (0, 4, 8, -1), (0, 2, 12, 2), (0, 1, 15, -2), (3, 1, 14, -2))

    def zb_copy(i):
        first, n, there, d = zb_parts[i]
        return copy(tok.at[pl.ds(first, n), x, yh, :, FIRST_SECOND], tok.at[pl.ds(there, n), x, yh, :, FIRST_SECOND],
                    zb_s.at[i], zb_r.at[i], {"blk": z_ids[d]})

    def yd_copy(row):
        part = tok.at[pl.ds(0, 4), x, row, :, THIRD]
        return copy(part, part, yd_s.at[0], yd_r.at[0], {"blk": y_id})

    def xd_copy(k, back=False):
        part = tok.at[pl.ds(0, 4), x_at[4 - k] if back else x, :, :, THIRD]
        return copy(part, part, xd_s.at[k - 1], xd_r.at[k - 1], {"blk": x_ids[k]})

    def zd_copy(i):
        first, n, there, d = zb_parts[i]
        return copy(tok.at[pl.ds(first, n), :, :, :, THIRD], tok.at[pl.ds(there, n), :, :, :, THIRD],
                    zd_s.at[i], zd_r.at[i], {"blk": z_ids[d]})

    def yb_copy(g, row):
        part = tok.at[pl.ds(4 * g, 4), x, row, :, FIRST]
        return copy(part, part, yb_s.at[g], yb_r.at[g], {"blk": y_id})

    def xc_copy(g, k, back=False):
        part = tok.at[pl.ds(4 * g, 4), x_at[4 - k] if back else x, yh, :, SECOND]
        return copy(part, part, xc_s.at[g, k - 1], xc_r.at[g, k - 1], {"blk": x_ids[k]})

    def xb_copy(g, k, back=False):
        part = tok.at[pl.ds(4 * g, 4), x_at[4 - k] if back else x, :, :, FIRST]
        return copy(part, part, xb_s.at[g, k - 1], xb_r.at[g, k - 1], {"blk": x_ids[k]})

    def yc_copy(g, row):
        part = tok.at[pl.ds(4 * g, 4), :, row, :, SECOND]
        return copy(part, part, yc_s.at[g], yc_r.at[g], {"blk": y_id})

    def tok_first():
        for k in (2, 1, 3):
            za_copy(k).start()
        zb_copy(3).start()

    def tok_near():
        for k in (1, 3, 2):
            za_copy(k).wait_recv()
        for i in (0, 1, 2, 4):
            zb_copy(i).start()
        yd_copy(yh).start()

    def tok_wide():
        yd_copy(1 - yh).wait_recv()
        for k in (1, 3, 2):
            xd_copy(k).start()

    def tok_far():
        for k in (1, 3, 2):
            xd_copy(k, back=True).wait_recv()
        for i in range(len(zb_parts)):
            zd_copy(i).start()

    def tok_second(g):
        for i, part in enumerate(zb_parts):
            if part[2] // 4 == g:
                zb_copy(i).wait_recv()
        for k in (1, 3, 2):
            xc_copy(g, k).start()
        yb_copy(g, yh).start()

    def tok_third(g):
        yb_copy(g, 1 - yh).wait_recv()
        for k in (1, 3, 2):
            xb_copy(g, k).start()
        for k in (1, 3, 2):
            xc_copy(g, k, back=True).wait_recv()
        yc_copy(g, yh).start()

    def tok_last(g):
        for k in (1, 3, 2):
            xb_copy(g, k, back=True).wait_recv()
        yc_copy(g, 1 - yh).wait_recv()
        for i, part in enumerate(zb_parts):
            if part[2] // 4 == g:
                zd_copy(i).wait_recv()

    each_role(emb_own)
    tok_first()
    each_role(emb_inner)
    tok_near()
    tok_second(0)
    each_role(emb_outer)
    tok_wide()

    goals = gb[...].reshape(NG * 8, W)
    premises = pb[...].reshape(NP * 8, W)
    s_own[...] = dot(premises, goals, NT)
    m1 = copy(s_own, s_in, m1_s.at[0], m1_r.at[0], {"mdl": 1 - m})
    m1.start()

    m1.wait_recv()
    scores = (s_own[...] + s_in[...]) * SCORE_SCALE
    top = jnp.max(scores, axis=0, keepdims=True)
    total = jnp.sum(jnp.exp(scores - top), axis=0, keepdims=True)
    line = lax.broadcasted_iota(jnp.int32, (8, 128), 0)
    stats[0] = jnp.where(line == 0, top, jnp.where(line == 1, total, lists))

    def l1_copy(k):
        return copy(stats.at[0], stats.at[k], l1_s.at[k - 1], l1_r.at[k - 1], {"blk": goal_ids[k]})

    for k in range(1, NG):
        l1_copy(k).start()
    tok_second(1)
    tok_second(2)
    tok_third(0)

    def gate_copy(c):
        return copy(gsend.at[c], gin.at[c], gu_s.at[c], gu_r.at[c], {"mdl": 1 - m})

    def gate_chunk(c):
        rows = tok[4 * c:4 * c + 4].reshape(256, W)
        both = dot(wgu_ref[...], rows, NT)
        gown[c] = both
        gsend[c] = both.astype(BF16)
        gate_copy(c).start()

    def spread(rows):
        lane = lax.broadcasted_iota(jnp.int32, (rows, 256), 1)
        sub = lax.broadcasted_iota(jnp.int32, (rows, 256), 0)
        return jnp.where(lax.rem(lax.div(lane, 8), 8) == lax.rem(sub, 8), 1.0, 0.0).astype(BF16)

    def act_chunk(c):
        gate_copy(c).wait_recv()
        g = gown[c, :U] + gin[c, :U].astype(F32)
        u = gown[c, U:] + gin[c, U:].astype(F32)
        s = 1.0 / (1.0 + jnp.exp(-g))
        a = g * s
        hidden = (a * u).astype(BF16)
        act1[c] = u * (s * (1.0 + g * (1.0 - s)))
        act2[c] = a
        part = dot(spread(8), hidden, NT)
        if c == 0:
            pool[:, U:] = jnp.zeros((8, 128 - U), F32)
            pool[:, :U] = part
        else:
            pool[:, :U] += part

    for k in range(1, NG):
        l1_copy(k).wait_recv()
    tops = [stats[k, 0:1] for k in range(NG)]
    peak = functools.reduce(jnp.maximum, tops)
    mass = functools.reduce(lambda p, q: p + q, [stats[k, 1:2] * jnp.exp(tops[k] - peak) for k in range(NG)])
    lse = peak + jnp.log(mass)
    codes = functools.reduce(lambda p, q: p + q, [stats[k] for k in range(NG)])
    count = codes[6:7]
    row = lax.broadcasted_iota(jnp.int32, (NP * 8, NG * 8), 0)
    member = lax.div(row, 8)
    premise_id = (blk_of(x, lax.div(member, 4), lax.rem(member, 4), zl) * 8 + lax.rem(row, 8)).astype(F32)
    weights = jnp.zeros((NP * 8, NG * 8), F32)
    for k in range(KPOS):
        hit = (codes[2 + k:3 + k] == premise_id) & (count > float(k))
        weights = weights + jnp.where(hit, 1.0, 0.0)
    coefficient = jnp.exp(scores - lse) - weights / count

    def mq_copy(role, k):
        src, dst = ((mbp, mbr), (mbp1, mbr1))[role]
        return copy(src.at[slot_of(role, k)], dst.at[k - 1], mq_s.at[k - 1], mq_r.at[k - 1], {"blk": ids_of(role)[k]})

    def r1_copy(role, k):
        first = (x_at, yh_at)[role][k] * 4
        return copy(go.at[pl.ds(first, 4)], rs1.at[k - 1], r1_s.at[k - 1], r1_r.at[k - 1], {"blk": ids_of(role)[4 * k]})

    def r2_copy(role, k):
        return copy(r2.at[(zl_at, zh_at)[role][k]], rs2.at[k - 1], r2_s.at[k - 1], r2_r.at[k - 1], {"blk": ids_of(role)[k]})

    def in_first(role):
        return (pslot, gslot)[role] == 0

    def start_sums(role):
        if role == 0:
            lhs = jnp.transpose(coefficient).astype(BF16)
            other = premises
        else:
            lhs = coefficient.astype(BF16)
            other = goals
        n = count_of(role)
        wide = W // n

        @pl.when(in_first(role))
        def _():
            target = (mbp, mbp1)[role]
            head = dot(lhs[:8], other, NN)
            for q in range(n):
                target[q] = head[:, q * wide:(q + 1) * wide]
            for k in range(1, n):
                mq_copy(role, k).start()

        go[:n] = dot(lhs, other, NN).astype(BF16).reshape(n, 8, W)
        for k in range(1, n // 4):
            r1_copy(role, k).start()

    each_role(start_sums)
    tok_second(3)
    tok_far()
    tok_third(1)

    def slice_of(role, q):
        wide = W // count_of(role)
        return mb.at[:, pl.ds(pl.multiple_of(q * wide, wide), wide)]

    def mp_copy(role, k):
        part = slice_of(role, slot_of(role, 0))
        return copy(part, part, mp_s.at[k - 1], mp_r.at[0], {"blk": ids_of(1 - role)[k]})

    def ma_copy(role, k, back=False):
        part = slice_of(role, slot_of(role, k if back else 0, back))
        return copy(part, part, ma_s.at[k - 1], ma_r.at[k - 1], {"blk": ids_of(role)[k]})

    def spread_micro(role):
        n = count_of(role)
        wide = W // n
        me = slot_of(role, 0)
        own, got = ((mbp, mbr), (mbp1, mbr1))[role]

        @pl.when(in_first(role))
        def _():
            acc = own[me]
            for k in range(1, n):
                mq_copy(role, k).wait_recv()
                acc = acc + got[k - 1]
            mb[:, pl.ds(pl.multiple_of(me * wide, wide), wide)] = ((GRAD_SCALE * acc) / SEQ).astype(BF16)
            for k in range(1, count_of(1 - role)):
                mp_copy(role, k).start()

        @pl.when(jnp.logical_not(in_first(role)))
        def _():
            mp_copy(role, 1).wait_recv()

        for k in range(1, n):
            ma_copy(role, k).start()

    each_role(spread_micro)
    tok_third(2)

    def second_sums(role):
        acc = go[pl.ds((x, yh)[role] * 4, 4)].astype(F32)
        for k in range(1, count_of(role) // 4):
            r1_copy(role, k).wait_recv()
            acc = acc + rs1[k - 1].astype(F32)
        r2[...] = acc.astype(BF16)
        for k in range(1, 4):
            r2_copy(role, k).start()

    each_role(second_sums)
    own_wg.wait()
    own_wu.wait()
    own_wd.wait()
    tok_last(0)
    gate_chunk(0)

    def all_micro(role):
        for k in range(1, count_of(role)):
            ma_copy(role, k, back=True).wait_recv()

    each_role(all_micro)
    bk_own[:, :U] = dot(mb[...], wd_ref[...], NT)
    bk_own[:, U:] = jnp.zeros((8, 128 - U), F32)
    back = copy(bk_own, bk_in, d_s.at[0], d_r.at[0], {"mdl": 1 - m})
    back.start()
    tok_third(3)
    tok_last(1)
    gate_chunk(1)

    def last_sums(role):
        acc = r2[(zl, zh)[role]].astype(F32)
        for k in range(1, 4):
            r2_copy(role, k).wait_recv()
            acc = acc + rs2[k - 1].astype(F32)
        eg_ref[...] = GRAD_SCALE * acc

    each_role(last_sums)
    act_chunk(0)
    back.wait_recv()
    back_rows = jnp.concatenate(thirds(jnp.transpose(bk_own[...] + bk_in[...])[:U]), axis=1)

    def back_chunk(c):
        wide = dot(back_rows, spread(24), NN)
        grads[:U, 256 * c:256 * c + 256] = (wide * act1[c]).astype(BF16)
        grads[U:, 256 * c:256 * c + 256] = (wide * act2[c]).astype(BF16)

    tok_last(2)
    gate_chunk(2)
    act_chunk(1)
    back_chunk(0)
    back_chunk(1)
    tok_last(3)
    gate_chunk(3)
    act_chunk(2)
    back_chunk(2)
    for j in range(W // TILE):
        cols = pl.ds(j * TILE, TILE)
        early[j] = dot(grads[:, :768], tok[:12, :, :, :, cols].reshape(768, TILE), NN)
    def drain(role):
        n = count_of(role)
        for k in range(1, 4):
            e1_copy(role, k).wait_send()
            r2_copy(role, k).wait_send()
        for o in range(1, n // 4):
            for i in range(4):
                e2_copy(role, o, i).wait_send()
            r1_copy(role, o).wait_send()
        for k in range(n):
            fw_copy(role, k).wait_send()
        for k in range(1, n):
            ma_copy(role, k).wait_send()

        @pl.when(in_first(role))
        def _():
            for k in range(1, n):
                mq_copy(role, k).wait_send()
            for k in range(1, count_of(1 - role)):
                mp_copy(role, k).wait_send()

    each_role(drain)
    for k in (1, 2, 3):
        za_copy(k).wait_send()
        xd_copy(k).wait_send()
    for i in range(len(zb_parts)):
        zb_copy(i).wait_send()
        zd_copy(i).wait_send()
    yd_copy(yh).wait_send()
    for g in range(4):
        yb_copy(g, yh).wait_send()
        yc_copy(g, yh).wait_send()
        for k in (1, 2, 3):
            xb_copy(g, k).wait_send()
            xc_copy(g, k).wait_send()
    m1.wait_send()
    back.wait_send()
    for k in range(1, NG):
        l1_copy(k).wait_send()
    for c in range(3):
        gate_copy(c).wait_send()

    act_chunk(3)
    back_chunk(3)
    pooled = jnp.concatenate(thirds(jnp.transpose(pool[...])[:U]), axis=1)
    gd_ref[...] = dot(pooled, jnp.concatenate([mb[...]] * 3, axis=0), NN).astype(BF16)
    for j in range(W // TILE):
        cols = pl.ds(j * TILE, TILE)
        both = early[j] + dot(grads[:, 768:], tok[12:, :, :, :, cols].reshape(256, TILE), NN)
        gg_ref[:, cols] = both[:U].astype(BF16)
        gu_ref[:, cols] = both[U:].astype(BF16)

    gate_copy(3).wait_send()


def hand_over(eg, gg, gu, gd, eg_out, gg_out, gu_out, gd_out, sem):
    copies = [pltpu.make_async_copy(eg, eg_out.at[0], sem.at[0])]
    for j in range(W // TILE):
        cols = pl.ds(j * TILE, TILE)
        for v, out in ((gg, gg_out), (gu, gu_out), (gd, gd_out)):
            copies.append(pltpu.make_async_copy(v.at[:, cols], out.at[0, :, cols], sem.at[len(copies)]))
    for c in copies:
        c.start()
    for c in copies:
        c.wait()


def on_device(embeddings, pos_index, pos_count, hidden_in, w_gate, w_up, w_down):
    vmem = pl.BlockSpec(memory_space=pltpu.VMEM)
    hbm = pl.BlockSpec(memory_space=pltpu.HBM)
    dma = pltpu.SemaphoreType.DMA
    shapes = [(5,), (3,), (3,), (3, 4), (3, 4), (16,), (16,), (1,), (1,), (15,), (15,), (3,), (3,), (3,), (3,)]
    shapes += [(15,), (15,), (15,), (1,), (15,), (15,), (1,), (1,)]
    shapes += [(3,), (3,), (5,), (5,), (4,), (4,), (4, 3), (4, 3), (4,), (4,), (4, 3), (4, 3), (1,), (1,), (3,), (3,), (5,), (5,), (4,), (4,)]
    results = (jax.ShapeDtypeStruct((1, 8, W), F32),) + (jax.ShapeDtypeStruct((1, U, W), BF16),) * 3
    parts = pl.pallas_call(
        kernel,
        out_shape=tuple(pltpu.VMEM(v.shape[1:], v.dtype) for v in results),
        in_specs=[vmem] * 2 + [hbm] * 5,
        out_specs=(vmem,) * 4,
        scratch_shapes=[
            pltpu.VMEM((8, W), BF16),
            pltpu.VMEM((8, 128), F32),
            pltpu.VMEM((2 * U, 1024), BF16),
            pltpu.VMEM((NZ, NX, NYH, 8, W), BF16),
            pltpu.VMEM((W // TILE, 2 * U, TILE), F32),
            pltpu.VMEM((NG, 8, W), BF16),
            pltpu.VMEM((NP, 8, W), BF16),
            pltpu.VMEM((2 * U, W), BF16),
            pltpu.VMEM((U, W), BF16),
            pltpu.VMEM((NP * 8, NG * 8), F32),
            pltpu.VMEM((NP * 8, NG * 8), F32),
            pltpu.VMEM((NG, 8, 128), F32),
            pltpu.VMEM((NG, 8, W), BF16),
            pltpu.VMEM((3, 4, 8, W), BF16),
            pltpu.VMEM((4, 8, W), BF16),
            pltpu.VMEM((3, 8, W), BF16),
            pltpu.VMEM((NG, 8, 128), F32),
            pltpu.VMEM((NG - 1, 8, 128), F32),
            pltpu.VMEM((NP, 8, 256), F32),
            pltpu.VMEM((NP - 1, 8, 256), F32),
            pltpu.VMEM((8, 128), F32),
            pltpu.VMEM((8, 128), F32),
            pltpu.VMEM((4, 2 * U, 256), F32),
            pltpu.VMEM((4, 2 * U, 256), BF16),
            pltpu.VMEM((4, 2 * U, 256), BF16),
            pltpu.VMEM((4, U, 256), F32),
            pltpu.VMEM((4, U, 256), F32),
        ]
        + [dma(s) for s in shapes],
        compiler_params=pltpu.CompilerParams(
            collective_id=0, has_side_effects=True, vmem_limit_bytes=60 * 1024 * 1024
        ),
    )(pos_index.T, pos_count[None], embeddings, hidden_in, w_gate, w_up, w_down)
    return pl.pallas_call(
        hand_over,
        out_shape=results,
        in_specs=[vmem] * 4,
        out_specs=(hbm,) * 4,
        scratch_shapes=[dma((13,))],
    )(*parts)


def solution(mesh):
    wide = P("tower", "blk", "mdl")
    return jax.shard_map(
        on_device,
        mesh=mesh,
        in_specs=(wide, P("blk", None), P("blk"), wide, wide, wide, wide),
        out_specs=(wide,) * 4,
        check_vma=False,
    )
```
